512 devices in a mesh: gx: 32 (over x, y, core), gy: 16 (over z).
Axes of the slice: x: 4, y: 4, z: 16, core: 2. Of those that a mesh axis runs over, the one named last changes fastest.
Arguments:
- right_side: float32 [2, 512, 2048], P(None, 'gx', 'gy'), may hold values from -160 to 160
- conductivity: float32 [512, 2048], P('gx', 'gy'), may hold values from 0.2 to 5
- leaf_inverse: float32 [128, 64, 128, 128], P('gx', 'gy'), may hold values from -1 to 4, as said below
- front_basis: float32 [512, 2048, 128], P('gx', 'gy'), may hold values from -0.25 to 0.25
- leaf_transfer: float32 [32, 16, 128, 128], P('gx', 'gy'), may hold values from -0.4375 to 0.4375
- node_transfer: float32 [32, 16, 8, 128, 128], P('gx', 'gy'), may hold values from -1 to 1, as said below
- leaf_front: float32 [32, 16, 128, 128], P('gx', 'gy'), may hold values from -1 to 1, as said below
- node_front: float32 [32, 16, 9, 128, 128], P('gx', 'gy'), may hold values from -1 to 1, as said below
Outputs:
- solution: float32 [2, 512, 2048], P(None, 'gx', 'gy')
- residual: float32 [2, 512, 2048], P(None, 'gx', 'gy')
- direction: float32 [2, 512, 2048], P(None, 'gx', 'gy')
The draws below stay inside these ranges and needn't reach their ends.
Inputs may be any that keep to these rules, and one draw needn't show every extreme that they name: `leaf_inverse`: every block is symmetric and positive definite. `leaf_front`: every matrix is symmetric and positive definite. `node_front`: every matrix is symmetric and positive definite; entry h - 1 is the same for all tiles covered by one node of level h. `node_transfer`: entry h - 1 is the same for all tiles covered by one node of level h.
All inputs are finite; a program needn't handle non-finite values.
Results may differ from the reference program's by a relative error of at most 0.0001.
Values sent between devices are 32-bit elements; how exact they have to be, the bound alone decides.
A program may use at most 64 MiB of HBM per device.

```python
import math
import jax
import jax.numpy as jnp
from jax import lax

CX = 16
CY = 128
RK = 128
LBX = 4
LBY = 32
RHS = 2
LEAF = 128
TILES_X = 32
TILES_Y = 16
TILES = 512
LEVELS = 9
NX = 512
NY = 2048
N_GX = 32
N_GY = 16


def dominant(key, shape, order, off_spread, low_diag, high_diag):
    first_key, second_key = jax.random.split(key)
    uniform_raw = jax.random.uniform(first_key, shape, jnp.float32, -1.0, 1.0)
    symmetric = 0.5 * (uniform_raw + jnp.swapaxes(uniform_raw, -1, -2)) * (off_spread / order)
    diagonal = jax.random.uniform(second_key, shape[:-1], jnp.float32, low_diag, high_diag)
    identity = jnp.eye(order, dtype=jnp.float32)
    return symmetric * (1.0 - identity) + identity * diagonal[..., None]


def draw_right_side(key, part):
    key_list = jax.random.split(jax.random.fold_in(key, 3), 3)
    row_log = jax.random.uniform(key_list[0], (NX,), jnp.float32, 0.0, 1.0)
    col_log = jax.random.uniform(key_list[1], (NY,), jnp.float32, 0.0, 1.0)
    row_place = jnp.arange(NX, dtype=jnp.float32) / max(NX - 1, 1)
    col_place = jnp.arange(NY, dtype=jnp.float32) / max(NY - 1, 1)
    row_scale = jnp.power(10.0, row_log - 0.5) * jnp.power(3.0, row_place - 0.5)
    col_scale = jnp.power(10.0, col_log - 0.5) * jnp.power(3.0, col_place - 0.5)
    scale_grid = row_scale[:, None] * col_scale[None, :]
    rough_part = jnp.clip(jax.random.normal(key_list[2], (RHS, NX, NY), jnp.float32), -5.0, 5.0)
    return rough_part * scale_grid[None, :, :]


def draw_leaf_inverse(key, part):
    return dominant(jax.random.fold_in(key, 5), (NX // LBX, NY // LBY, LEAF, LEAF), LEAF, 1.5, 1.6, 3.2)


def draw_leaf_front(key, part):
    return dominant(jax.random.fold_in(key, 7), (TILES_X, TILES_Y, RK, RK), RK, 0.2, 0.25, 0.5)


def draw_node_transfer(key, part):
    scale = (RK * 7 // 5) ** (-0.5)
    stacked = []
    for height in range(1, LEVELS):
        level_key = jax.random.fold_in(jax.random.fold_in(key, 13), height)
        nodes = jnp.clip(jax.random.normal(level_key, (TILES >> height, RK, RK), jnp.float32), -4.0, 4.0) * scale
        stacked.append(jnp.repeat(nodes, 1 << height, axis=0))
    return jnp.stack(stacked, axis=1).reshape(TILES_X, TILES_Y, LEVELS - 1, RK, RK)


def draw_node_front(key, part):
    stacked = []
    for height in range(1, LEVELS + 1):
        level_key = jax.random.fold_in(jax.random.fold_in(key, 11), height)
        nodes = dominant(level_key, (TILES >> height, RK, RK), RK, 0.2, 0.25, 0.5)
        stacked.append(jnp.repeat(nodes, 1 << height, axis=0))
    return jnp.stack(stacked, axis=1).reshape(TILES_X, TILES_Y, LEVELS, RK, RK)


def shard_levels(key, extent, cuts, least, largest):
    def one(axis_at, blocks):
        draws = jax.random.uniform(jax.random.fold_in(jax.random.fold_in(key, 6), axis_at), (blocks,), jnp.float32, least / len(cuts), largest / len(cuts))
        return jnp.repeat(jnp.exp(draws), extent[axis_at] // blocks).reshape((-1,) + (1,) * (len(extent) - axis_at - 1))

    factor_of = one(*cuts[0])
    for cut in cuts[1:]:
        factor_of = factor_of * one(*cut)
    return factor_of


def bell_draw(stream_key, extent, width, reach, cuts=(), held_as=jnp.bfloat16):
    values = jax.random.normal(stream_key, extent, jnp.float32) * width
    if len(cuts) > 0:
        values = shard_levels(stream_key, extent, cuts, -0.22, 0.18) * values
    return jnp.clip(values, min=-reach, max=reach).astype(held_as)


def setup_inputs(seed: int = 0) -> dict:
    splits = jax.random.split(jax.random.key(seed), 9)
    right_side = draw_right_side(jax.random.fold_in(splits[8], 71), 0)
    conductivity = jnp.clip(jnp.exp(math.log(5.0) - 3.218876 * jax.random.uniform(splits[1], (NX, NY), jnp.float32) ** shard_levels(splits[1], (NX, NY), ((0, 32), (1, 16)), -0.2, 0.2)), 0.2, 5.0)
    leaf_inverse = draw_leaf_inverse(jax.random.fold_in(splits[8], 71), 0)
    front_basis = bell_draw(splits[3], (NX, NY, RK), (CX * CY // 4) ** -0.5, 0.25, ((0, 32), (1, 16)), jnp.float32)
    leaf_transfer = bell_draw(splits[4], (TILES_X, TILES_Y, RK, RK), (RK * 7 // 5) ** -0.5, 0.4375, ((0, 32), (1, 16)), jnp.float32)
    node_transfer = draw_node_transfer(jax.random.fold_in(splits[8], 71), 0)
    leaf_front = draw_leaf_front(jax.random.fold_in(splits[8], 71), 0)
    node_front = draw_node_front(jax.random.fold_in(splits[8], 71), 0)
    return {"right_side": right_side, "conductivity": conductivity, "leaf_inverse": leaf_inverse, "front_basis": front_basis, "leaf_transfer": leaf_transfer, "node_transfer": node_transfer, "leaf_front": leaf_front, "node_front": node_front}


HIGHEST = lax.Precision.HIGHEST


def operate_padded(padded, padded_k):
    extent_x = padded.shape[1] - 2
    extent_y = padded.shape[2] - 2
    center = padded[:, 1:-1, 1:-1]
    center_k = padded_k[1:-1, 1:-1]
    summed = jnp.zeros_like(center)
    for offset_x, offset_y in ((2, 1), (0, 1), (1, 2), (1, 0)):
        beside = padded[:, offset_x:offset_x + extent_x, offset_y:offset_y + extent_y]
        beside_k = padded_k[offset_x:offset_x + extent_x, offset_y:offset_y + extent_y]
        summed = summed + 0.5 * (center_k + beside_k) * (center - beside)
    return summed


def operate(values, conduct):
    padded = jnp.pad(values, ((0, 0), (1, 1), (1, 1)))
    padded_k = jnp.pad(conduct, ((1, 1), (1, 1)))
    return operate_padded(padded, padded_k)


def leaf_apply(values, leaf_inverse):
    count_s, extent_x, extent_y = values.shape
    blocks_x = extent_x // LBX
    blocks_y = extent_y // LBY
    grouped = values.reshape(count_s, blocks_x, LBX, blocks_y, LBY).transpose(0, 1, 3, 2, 4)
    grouped = grouped.reshape(count_s, blocks_x, blocks_y, LBX * LBY)
    mapped = jnp.einsum("xyij,sxyj->sxyi", leaf_inverse, grouped, precision=HIGHEST)
    mapped = mapped.reshape(count_s, blocks_x, blocks_y, LBX, LBY).transpose(0, 1, 3, 2, 4)
    return mapped.reshape(count_s, extent_x, extent_y)


def tree_apply(coeffs, leaf_transfer, node_transfer, leaf_front, node_front):
    devices = coeffs.shape[0]
    levels = devices.bit_length() - 1
    leaf_t = leaf_transfer.reshape(devices, RK, RK)
    node_t = node_transfer.reshape(devices, levels - 1, RK, RK)
    leaf_f = leaf_front.reshape(devices, RK, RK)
    node_f = node_front.reshape(devices, levels, RK, RK)
    uppers = [coeffs]
    moving = jnp.einsum("dsj,djk->dsk", coeffs, leaf_t, precision=HIGHEST)
    uppers.append(moving[0::2] + moving[1::2])
    for height in range(2, levels + 1):
        owners = jnp.arange(devices >> (height - 1), dtype=jnp.int32) * (1 << (height - 1))
        moving = jnp.einsum("dsj,djk->dsk", uppers[height - 1], node_t[owners, height - 2], precision=HIGHEST)
        uppers.append(moving[0::2] + moving[1::2])
    downward = jnp.einsum("dsj,jk->dsk", uppers[levels], node_f[0, levels - 1], precision=HIGHEST)
    for height in range(levels, 1, -1):
        owners = jnp.arange(devices >> (height - 1), dtype=jnp.int32) * (1 << (height - 1))
        parents = jnp.repeat(downward, 2, axis=0)
        downward = jnp.einsum("dsk,djk->dsj", parents, node_t[owners, height - 2], precision=HIGHEST) + jnp.einsum(
            "dsj,djk->dsk", uppers[height - 1], node_f[owners, height - 2], precision=HIGHEST)
    parents = jnp.repeat(downward, 2, axis=0)
    return jnp.einsum("dsk,djk->dsj", parents, leaf_t, precision=HIGHEST) + jnp.einsum(
        "dsj,djk->dsk", coeffs, leaf_f, precision=HIGHEST)


def precondition(values, leaf_inverse, front_basis, leaf_transfer, node_transfer, leaf_front, node_front):
    count_s = values.shape[0]
    near = leaf_apply(values, leaf_inverse)
    tiles = values.reshape(count_s, N_GX, CX, N_GY, CY)
    basis_tiles = front_basis.reshape(N_GX, CX, N_GY, CY, RK)
    coeffs = jnp.einsum("sxayb,xaybk->xysk", tiles, basis_tiles, precision=HIGHEST)
    coeffs = coeffs.reshape(N_GX * N_GY, count_s, RK)
    spread = tree_apply(coeffs, leaf_transfer, node_transfer, leaf_front, node_front)
    spread_t = spread.reshape(N_GX, N_GY, count_s, RK)
    far = jnp.einsum("xysk,xaybk->sxayb", spread_t, basis_tiles, precision=HIGHEST)
    return near + far.reshape(values.shape)


def reference(right_side, conductivity, leaf_inverse, front_basis, leaf_transfer, node_transfer, leaf_front, node_front):
    def apply_inverse(values):
        return precondition(values, leaf_inverse, front_basis, leaf_transfer, node_transfer, leaf_front, node_front)

    first_z = apply_inverse(right_side)
    rz_old = jnp.sum(right_side * first_z, axis=(1, 2))
    applied = operate(first_z, conductivity)
    curvature = jnp.sum(first_z * applied, axis=(1, 2))
    step_size = (rz_old / curvature)[:, None, None]
    solution = step_size * first_z
    residual = right_side - step_size * applied
    second_z = apply_inverse(residual)
    rz_new = jnp.sum(residual * second_z, axis=(1, 2))
    direction = second_z + (rz_new / rz_old)[:, None, None] * first_z
    return (solution, residual, direction)
```

```python
import jax
import jax.numpy as jnp
from jax import lax
from jax.experimental import pallas as pl
from jax.experimental.pallas import tpu as pltpu
from jax.sharding import PartitionSpec as P

HIGHEST = lax.Precision.HIGHEST
MESH = pl.DeviceIdType.MESH
F32 = jnp.float32
K = 128


def dot(a, b):
    return lax.dot_general(
        a, b, (((1,), (0,)), ((), ())), precision=HIGHEST, preferred_element_type=F32
    )


def dot_t(a, b):
    return lax.dot_general(
        a, b, (((1,), (1,)), ((), ())), precision=HIGHEST, preferred_element_type=F32
    )


def units(extra):
    return {d: 5 - d.bit_length() + extra for d in range(1, 16)}


def offsets(count):
    at, out = 0, {}
    for d in sorted(count):
        out[d] = at
        at += count[d]
    return out, at


def butterfly(values):
    while len(values) > 1:
        values = [values[i] + values[i + 1] for i in range(0, len(values), 2)]
    return values[0]


ORDER = (8, 15, 14, 13, 12, 11, 10, 9, 7, 6, 5, 4, 3, 2, 1)


def tile_rows(x):
    return jnp.concatenate([x, x], axis=0)


def shuffle(t):
    row = lax.broadcasted_iota(jnp.int32, t.shape, 0) % 4
    chunk = lax.broadcasted_iota(jnp.int32, t.shape, 1) // 32
    rows, lanes = t.shape
    out = t
    for delta in (-3, -2, -1, 1, 2, 3):
        moved = pltpu.roll(t, delta % rows, 0)
        moved = pltpu.roll(moved, (-32 * delta) % lanes, 1)
        out = jnp.where(row - chunk == delta, moved, out)
    return out


def kernel(
    rs_h, cond_h, linv_h, basis_h, e0_h, nt_h, f0_h, nf_h,
    sol_o, res_o, dir_o,
    rs, cond, linv, basis, e0, nt, f0, nf,
    pu, ru, gs, lb, wt, tmp,
    zs1, zb1, zs2, zb2, zs3, zb3,
    cs1, cb1, cs2, cb2, cs3, cb3,
    gs1, gb1, gs2, gb2, gs3, gb3,
    hrs, hrb, hcs, hcb, krs, krb, kcs, kcb,
    lsem, ssem, rsem, hsem, hrsem,
):
    X = lax.axis_index("gx")
    Z = lax.axis_index("gy")
    z_peer = lambda d: (X, Z ^ d)
    c_peer = (X ^ 1, Z)
    g_peer = lambda d: (X ^ (2 * d), Z)
    x_up, x_down = (X + 1) % 32, (X + 31) % 32
    z_up, z_down = (Z + 1) % 16, (Z + 15) % 16

    barrier = pltpu.get_barrier_semaphore()
    others = [z_peer(d) for d in ORDER] + [g_peer(d) for d in ORDER] + [c_peer]
    halo = [(x_up, Z), (x_down, Z), (X, z_up), (X, z_down)]
    for who in others + halo:
        pl.semaphore_signal(barrier, inc=1, device_id=who, device_id_type=MESH)

    loads = {}
    for i, (name, src, dst) in enumerate(
        (
            ("e0", e0_h.at[0, 0], e0),
            ("nt", nt_h.at[0, 0], nt),
            ("rs", rs_h, rs),
            ("basis", basis_h, basis),
            ("cond", cond_h, cond),
            ("f0", f0_h.at[0, 0], f0),
            ("nf", nf_h.at[0, 0], nf),
            ("linv", linv_h, linv),
        )
    ):
        loads[name] = pltpu.make_async_copy(src, dst, lsem.at[i])
        loads[name].start()

    def send(src, dst, sends, recvs, who):
        copy = pltpu.make_async_remote_copy(
            src_ref=src, dst_ref=dst, send_sem=sends, recv_sem=recvs,
            device_id=who, device_id_type=MESH,
        )
        copy.start()
        return copy

    def send_group(src, buf, extra, slot, peer):
        count = units(extra)
        at, _ = offsets(count)
        for d in ORDER:
            n = count[d]
            send(
                src.at[pl.ds(0, n)], buf.at[pl.ds(at[d], n)], ssem.at[slot], rsem.at[slot], peer(d)
            )

    def wait_bytes(buf, sem):
        pltpu.make_async_copy(buf, buf, sem).wait()

    def group_sums(src, buf, extra):
        count = units(extra)
        at, _ = offsets(count)
        out = []
        for unit in range(4 + extra):
            reach = [d for d in range(1, 16) if count[d] > unit]
            out.append(butterfly([src[unit]] + [buf[at[d] + unit] for d in reach]))
        return out

    row = lax.broadcasted_iota(jnp.int32, (32, K), 0)
    lane = lax.broadcasted_iota(jnp.int32, (32, K), 1)

    def send_edges(t, rows_src, rows_buf, cols_src, cols_buf, first):
        rows_src[0] = jnp.concatenate([t[15:16], t[31:32]], axis=0)
        rows_src[1] = jnp.concatenate([t[0:1], t[16:17]], axis=0)
        lane8 = lane[0:8]
        last_col = pltpu.roll(t[0:8], 1, 1)
        first_col = t[0:8]
        for j in range(1, 4):
            part = t[8 * j : 8 * j + 8]
            last_col = jnp.where(lane8 == j, pltpu.roll(part, j + 1, 1), last_col)
            first_col = jnp.where(lane8 == j, pltpu.roll(part, j, 1), first_col)
        cols_src[0] = last_col
        cols_src[1] = first_col
        return [
            send(rows_src.at[0], rows_buf.at[0], hsem.at[first], hrsem.at[first], (x_up, Z)),
            send(rows_src.at[1], rows_buf.at[1], hsem.at[first + 1], hrsem.at[first + 1], (x_down, Z)),
            send(cols_src.at[0], cols_buf.at[0], hsem.at[first + 2], hrsem.at[first + 2], (X, z_up)),
            send(cols_src.at[1], cols_buf.at[1], hsem.at[first + 3], hrsem.at[first + 3], (X, z_down)),
        ]

    def beside(t, rows_buf, cols_buf):
        def spread(h):
            return jnp.concatenate(
                [jnp.broadcast_to(h[0:1], (16, K)), jnp.broadcast_to(h[1:2], (16, K))], axis=0
            )

        low = spread(jnp.where(X > 0, rows_buf[0], 0.0))
        high = spread(jnp.where(X < 31, rows_buf[1], 0.0))
        left = jnp.where(Z > 0, cols_buf[0], 0.0)
        right = jnp.where(Z < 15, cols_buf[1], 0.0)
        left = jnp.concatenate([left] + [pltpu.roll(left, K - j, 1) for j in range(1, 4)], axis=0)
        right = jnp.concatenate([pltpu.roll(right, K - 1 - j, 1) for j in range(4)], axis=0)
        return (
            jnp.where(row % 16 == 15, high, pltpu.roll(t, 31, 0)),
            jnp.where(row % 16 == 0, low, pltpu.roll(t, 1, 0)),
            jnp.where(lane == K - 1, right, pltpu.roll(t, K - 1, 1)),
            jnp.where(lane == 0, left, pltpu.roll(t, 1, 1)),
        )

    def flat_rows(ref):
        return jnp.concatenate([ref[:, x, :] for x in range(16)], axis=1)

    def coefficients(ref):
        return dot(flat_rows(ref), basis[...].reshape(16 * K, K))

    def leaf_apply(t):
        g = shuffle(t)
        for i in range(16):
            lhs = jnp.concatenate([g[i : i + 1], g[16 + i : 17 + i]], axis=0)
            out = dot(lhs, linv[i // 4, i % 4])
            tmp[pl.ds(i, 1)] = out[0:1]
            tmp[pl.ds(16 + i, 1)] = out[1:2]
        return shuffle(tmp[...])

    def spread_out(y):
        w = dot_t(y, basis[...].reshape(16 * K, K))
        for x in range(16):
            wt[:, x, :] = w[:, x * K : (x + 1) * K]
        return wt[...].reshape(32, K)

    def put(ref, rows2, first=0):
        for i in range(rows2.shape[1] // K):
            ref[first + i] = rows2[:, i * K : (i + 1) * K]

    loads["e0"].wait()
    loads["nt"].wait()
    p = e0[...]
    pu[:, 3 * K : 4 * K] = p
    for i in range(3):
        p = dot(p, nt[i])
        pu[:, (2 - i) * K : (3 - i) * K] = p
    loads["rs"].wait()
    loads["basis"].wait()
    u0 = coefficients(rs)
    put(zs1, dot(u0, pu[...]))
    pl.semaphore_wait(barrier, len(others) + len(halo))
    send_group(zs1, zb1, 0, 0, z_peer)

    loads["cond"].wait()
    k32 = tile_rows(cond[...])
    edges_k = send_edges(k32, krs, krb, kcs, kcb, 0)
    r = nt[3]
    ru[:, 4 * K : 5 * K] = r
    for i in range(4):
        r = dot(r, nt[4 + i])
        ru[:, (3 - i) * K : (4 - i) * K] = r
    loads["f0"].wait()
    loads["nf"].wait()
    gs[0:K] = f0[...]
    for h in range(1, 5):
        gs[h * K : (h + 1) * K] = dot_t(nf[h - 1], pu[:, (4 - h) * K : (5 - h) * K])
    loads["linv"].wait()
    b32 = rs[...].reshape(32, K)
    lb[...] = leaf_apply(b32)

    def up_z(buf, src, extra, slot):
        wait_bytes(buf, rsem.at[slot])
        return group_sums(src, buf, extra)

    def core_round(src, buf, slot):
        copy = send(src, buf, ssem.at[slot], rsem.at[slot], c_peer)
        copy.wait_recv()
        return copy, src[...] + buf[...]

    u4, u3, u2, u1 = up_z(zb1, zs1, 0, 0)
    put(cs1, dot(u4, ru[...]))
    core1, c = core_round(cs1, cb1, 1)
    u5 = c[4]
    gs1[...] = c[0:4]
    send_group(gs1, gb1, 0, 2, g_peer)
    for h in range(5, 10):
        g = dot_t(nf[h - 1], ru[:, (9 - h) * K : (10 - h) * K])
        gs[h * K : (h + 1) * K] = dot_t(g, pu[:, 0:K])
    y = dot(jnp.concatenate([u0, u1, u2, u3, u4, u5], axis=1), gs[0 : 6 * K])
    for e in edges_k:
        e.wait_recv()
    weights = [0.5 * (k32 + other) for other in beside(k32, krb, kcb)]
    u9, u8, u7, u6 = up_z(gb1, gs1, 0, 2)
    y = y + dot(jnp.concatenate([u6, u7, u8, u9], axis=1), gs[6 * K : 10 * K])
    z = lb[...] + spread_out(y)

    edges_z = send_edges(z, hrs, hrb, hcs, hcb, 4)
    for e in edges_z:
        e.wait_recv()
    applied = jnp.zeros_like(z)
    for weight, other in zip(weights, beside(z, hrb, hcb)):
        applied = applied + weight * (z - other)
    res_o[...] = applied.reshape(2, 16, K)

    def total(t):
        return jnp.sum(t.reshape(2, 16, K), axis=(1, 2), keepdims=True)[:, 0]

    lane2 = lane[0:2]
    u0 = coefficients(res_o)
    zs2[0] = jnp.where(
        lane2 == 0, total(b32 * z), jnp.where(lane2 == 1, total(z * applied), 0.0)
    )
    put(zs2, dot(u0, pu[...]), 1)
    send_group(zs2, zb2, 1, 3, z_peer)
    near = leaf_apply(applied)
    s0, u4, u3, u2, u1 = up_z(zb2, zs2, 1, 3)
    cs2[0] = s0
    put(cs2, dot(u4, ru[...]), 1)
    core2, c = core_round(cs2, cb2, 4)
    u5 = c[5]
    gs2[...] = c[0:5]
    send_group(gs2, gb2, 1, 5, g_peer)
    y = dot(jnp.concatenate([u0, u1, u2, u3, u4, u5], axis=1), gs[0 : 6 * K])
    s0, u9, u8, u7, u6 = up_z(gb2, gs2, 1, 5)
    y = y + dot(jnp.concatenate([u6, u7, u8, u9], axis=1), gs[6 * K : 10 * K])
    mapped = near + spread_out(y)

    rz_old = s0[:, 0:1]
    step = rz_old / s0[:, 1:2]
    step32 = jnp.concatenate(
        [jnp.broadcast_to(step[0:1], (16, K)), jnp.broadcast_to(step[1:2], (16, K))], axis=0
    )
    residual = b32 - step32 * applied
    second = z - step32 * mapped
    zs3[0] = jnp.broadcast_to(total(residual * second), (2, K))
    for d in ORDER:
        send(zs3, zb3.at[pl.ds(d - 1, 1)], ssem.at[6], rsem.at[6], z_peer(d))
    sol_o[...] = (step32 * z).reshape(2, 16, K)
    res_o[...] = residual.reshape(2, 16, K)
    wait_bytes(zb3, rsem.at[6])
    cs3[0] = butterfly([zs3[0]] + [zb3[d] for d in range(15)])
    core3, c = core_round(cs3, cb3, 7)
    gs3[...] = c
    for d in ORDER:
        send(gs3, gb3.at[pl.ds(d - 1, 1)], ssem.at[8], rsem.at[8], g_peer(d))
    wait_bytes(gb3, rsem.at[8])
    rz_new = butterfly([gs3[0]] + [gb3[d] for d in range(15)])
    ratio = rz_new / rz_old
    ratio32 = jnp.concatenate(
        [jnp.broadcast_to(ratio[0:1], (16, K)), jnp.broadcast_to(ratio[1:2], (16, K))], axis=0
    )
    dir_o[...] = (second + ratio32 * z).reshape(2, 16, K)

    for e in edges_k + edges_z + [core1, core2, core3]:
        e.wait_send()
    for buf, slot in ((zb1, 0), (gb1, 2), (zb2, 3), (gb2, 5), (zb3, 6), (gb3, 8)):
        wait_bytes(buf, ssem.at[slot])


def on_device(*args):
    unit = lambda n: pltpu.VMEM((n, 2, K), F32)
    square = lambda *n: pltpu.VMEM(n + (K, K), F32)
    out = jax.ShapeDtypeStruct((2, 16, K), F32)
    return pl.pallas_call(
        kernel,
        name="pcg_step",
        out_shape=(out, out, out),
        in_specs=[pl.BlockSpec(memory_space=pl.ANY)] * 8,
        out_specs=[pl.BlockSpec(memory_space=pltpu.VMEM)] * 3,
        scratch_shapes=[
            pltpu.VMEM((2, 16, K), F32), pltpu.VMEM((16, K), F32), square(4, 4), square(16),
            square(), square(8), square(), square(9),
            pltpu.VMEM((K, 4 * K), F32), pltpu.VMEM((K, 5 * K), F32), pltpu.VMEM((10 * K, K), F32),
            pltpu.VMEM((32, K), F32), pltpu.VMEM((2, 16, K), F32), pltpu.VMEM((32, K), F32),
            unit(4), unit(26), unit(5), unit(41), unit(1), unit(15),
            unit(5), unit(5), unit(6), unit(6), unit(1), unit(1),
            unit(4), unit(26), unit(5), unit(41), unit(1), unit(15),
            unit(2), unit(2), pltpu.VMEM((2, 8, K), F32), pltpu.VMEM((2, 8, K), F32),
            unit(2), unit(2), pltpu.VMEM((2, 8, K), F32), pltpu.VMEM((2, 8, K), F32),
            pltpu.SemaphoreType.DMA((8,)), pltpu.SemaphoreType.DMA((9,)),
            pltpu.SemaphoreType.DMA((9,)), pltpu.SemaphoreType.DMA((8,)),
            pltpu.SemaphoreType.DMA((8,)),
        ],
        compiler_params=pltpu.CompilerParams(
            collective_id=0, has_side_effects=True, vmem_limit_bytes=60 * 1024 * 1024
        ),
    )(*args)


def solution(mesh):
    return jax.shard_map(
        on_device,
        mesh=mesh,
        in_specs=(
            P(None, "gx", "gy"),
            P("gx", "gy"),
            P("gx", "gy", None, None),
            P("gx", "gy", None),
            P("gx", "gy", None, None),
            P("gx", "gy", None, None, None),
            P("gx", "gy", None, None),
            P("gx", "gy", None, None, None),
        ),
        out_specs=(P(None, "gx", "gy"), P(None, "gx", "gy"), P(None, "gx", "gy")),
        check_vma=False,
    )
```

```python
import jax
import jax.numpy as jnp
from jax import lax
from jax.experimental import pallas as pl
from jax.experimental.pallas import tpu as pltpu
from jax.sharding import PartitionSpec as P

HIGHEST = lax.Precision.HIGHEST
MESH = pl.DeviceIdType.MESH
F32 = jnp.float32
BF16 = jnp.bfloat16
K = 128


def dot(a, b):
    return lax.dot_general(
        a, b, (((1,), (0,)), ((), ())), precision=HIGHEST, preferred_element_type=F32
    )


def dot_t(a, b):
    return lax.dot_general(
        a, b, (((1,), (1,)), ((), ())), precision=HIGHEST, preferred_element_type=F32
    )


def halves(a):
    high = a.astype(BF16)
    return high, (a - high.astype(F32)).astype(BF16)


def both(a):
    return jnp.concatenate(halves(a), axis=0)


def fold(out):
    n = out.shape[0] // 2
    return out[0:n] + out[n:]


def dot_w(a, w):
    n = w.shape[1] // 2
    out = fold(jnp.dot(both(a), w, preferred_element_type=F32))
    return out[:, 0:n] + out[:, n:]


def units():
    return {d: 5 - d.bit_length() for d in range(1, 16)}


def offsets(count):
    at, out = 0, {}
    for d in sorted(count):
        out[d] = at
        at += count[d]
    return out, at


def butterfly(values):
    while len(values) > 1:
        values = [values[i] + values[i + 1] for i in range(0, len(values), 2)]
    return values[0]


ORDER = (8, 15, 14, 13, 12, 11, 10, 9, 7, 6, 5, 4, 3, 2, 1)


def tile_rows(x):
    return jnp.concatenate([x, x], axis=0)


def shuffle(t):
    row = lax.broadcasted_iota(jnp.int32, t.shape, 0) % 4
    chunk = lax.broadcasted_iota(jnp.int32, t.shape, 1) // 32
    rows, lanes = t.shape
    out = t
    for delta in (-3, -2, -1, 1, 2, 3):
        moved = pltpu.roll(t, delta % rows, 0)
        moved = pltpu.roll(moved, (-32 * delta) % lanes, 1)
        out = jnp.where(row - chunk == delta, moved, out)
    return out


def kernel(
    rs_h, cond_h, linv_h, basis_h, e0_h, nt_h, f0_h, nf_h,
    sol_o, res_o, dir_o,
    rs, cond, linv, basis, e0, nt, f0, nf,
    pf, rf, basis2, linv2, pa, pb, ra, rb, gs, lb, wt, tmp,
    zs1, zb1, zs2, zb2, cs1, cb1, cs2, cb2, gs1, gb1, gs2, gb2,
    hrs, hrb, hcs, hcb, krs, krb, kcs, kcb,
    lsem, ssem, rsem, hsem, hrsem,
):
    X = lax.axis_index("gx")
    Z = lax.axis_index("gy")
    z_peer = lambda d: (X, Z ^ d)
    c_peer = (X ^ 1, Z)
    g_peer = lambda d: (X ^ (2 * d), Z)
    x_up, x_down = (X + 1) % 32, (X + 31) % 32
    z_up, z_down = (Z + 1) % 16, (Z + 15) % 16

    loads = {}
    parts = [
        ("e0", e0_h.at[0, 0], e0),
        ("nt0", nt_h.at[0, 0, pl.ds(0, 3)], nt.at[pl.ds(0, 3)]),
        ("rs", rs_h, rs),
    ]
    for i in range(4):
        at = pl.ds(4 * i, 4)
        parts.append(("basis%d" % i, basis_h.at[at], basis.at[at]))
    parts += [
        ("nt1", nt_h.at[0, 0, pl.ds(3, 5)], nt.at[pl.ds(3, 5)]),
        ("cond", cond_h, cond),
        ("nf", nf_h.at[0, 0], nf),
        ("linv", linv_h, linv),
        ("f0", f0_h.at[0, 0], f0),
    ]
    for i, (name, src, dst) in enumerate(parts):
        loads[name] = pltpu.make_async_copy(src, dst, lsem.at[i])
        loads[name].start()

    barrier = pltpu.get_barrier_semaphore()
    others = [z_peer(d) for d in ORDER] + [g_peer(d) for d in ORDER] + [c_peer]
    halo = [(x_up, Z), (x_down, Z), (X, z_up), (X, z_down)]
    for who in others + halo:
        pl.semaphore_signal(barrier, inc=1, device_id=who, device_id_type=MESH)

    def send(src, dst, sends, recvs, who):
        copy = pltpu.make_async_remote_copy(
            src_ref=src, dst_ref=dst, send_sem=sends, recv_sem=recvs,
            device_id=who, device_id_type=MESH,
        )
        copy.start()
        return copy

    def send_group(src, buf, slot, peer):
        count = units()
        at, _ = offsets(count)
        for d in ORDER:
            n = count[d]
            send(
                src.at[pl.ds(0, n)], buf.at[pl.ds(at[d], n)], ssem.at[slot], rsem.at[slot], peer(d)
            )

    def send_all(src, buf, slot, peer):
        for d in ORDER:
            send(src, buf.at[d - 1], ssem.at[slot], rsem.at[slot], peer(d))

    def wait_bytes(buf, sem):
        pltpu.make_async_copy(buf, buf, sem).wait()

    def group_sums(src, buf):
        count = units()
        at, _ = offsets(count)
        out = []
        for unit in range(4):
            reach = [d for d in range(1, 16) if count[d] > unit]
            out.append(butterfly([src[unit]] + [buf[at[d] + unit] for d in reach]))
        return out

    def all_sums(src, buf, unit, size):
        terms = [src[unit]] + [buf[d, unit] for d in range(15)]
        return [butterfly(terms[i : i + size]) for i in range(0, 16, size)]

    def products(src, buf, unit, other, size):
        sums = all_sums(src, buf, unit, size)
        images = all_sums(src, buf, other, size)
        return sums[0], butterfly([s * m for s, m in zip(sums, images)])

    row = lax.broadcasted_iota(jnp.int32, (32, K), 0)
    lane = lax.broadcasted_iota(jnp.int32, (32, K), 1)

    def send_edges(t, rows_src, rows_buf, cols_src, cols_buf, first):
        rows_src[0] = jnp.concatenate([t[15:16], t[31:32]], axis=0)
        rows_src[1] = jnp.concatenate([t[0:1], t[16:17]], axis=0)
        lane8 = lane[0:8]
        last_col = pltpu.roll(t[0:8], 1, 1)
        first_col = t[0:8]
        for j in range(1, 4):
            part = t[8 * j : 8 * j + 8]
            last_col = jnp.where(lane8 == j, pltpu.roll(part, j + 1, 1), last_col)
            first_col = jnp.where(lane8 == j, pltpu.roll(part, j, 1), first_col)
        cols_src[0] = last_col
        cols_src[1] = first_col
        return [
            send(rows_src.at[0], rows_buf.at[0], hsem.at[first], hrsem.at[first], (x_up, Z)),
            send(rows_src.at[1], rows_buf.at[1], hsem.at[first + 1], hrsem.at[first + 1], (x_down, Z)),
            send(cols_src.at[0], cols_buf.at[0], hsem.at[first + 2], hrsem.at[first + 2], (X, z_up)),
            send(cols_src.at[1], cols_buf.at[1], hsem.at[first + 3], hrsem.at[first + 3], (X, z_down)),
        ]

    def beside(t, rows_buf, cols_buf):
        def spread(h):
            return jnp.concatenate(
                [jnp.broadcast_to(h[0:1], (16, K)), jnp.broadcast_to(h[1:2], (16, K))], axis=0
            )

        low = spread(jnp.where(X > 0, rows_buf[0], 0.0))
        high = spread(jnp.where(X < 31, rows_buf[1], 0.0))
        left = jnp.where(Z > 0, cols_buf[0], 0.0)
        right = jnp.where(Z < 15, cols_buf[1], 0.0)
        left = jnp.concatenate([left] + [pltpu.roll(left, K - j, 1) for j in range(1, 4)], axis=0)
        right = jnp.concatenate([pltpu.roll(right, K - 1 - j, 1) for j in range(4)], axis=0)
        return (
            jnp.where(row % 16 == 15, high, pltpu.roll(t, 31, 0)),
            jnp.where(row % 16 == 0, low, pltpu.roll(t, 1, 0)),
            jnp.where(lane == K - 1, right, pltpu.roll(t, K - 1, 1)),
            jnp.where(lane == 0, left, pltpu.roll(t, 1, 1)),
        )

    def flat_rows(ref):
        return jnp.concatenate([ref[:, x, :] for x in range(16)], axis=1)

    def coefficients(ref):
        return dot_w(flat_rows(ref), basis2[...])

    def leaf_apply(t):
        high, low = halves(shuffle(t))
        high, low = high.astype(F32), low.astype(F32)
        for i in range(16):
            j = 16 + i
            lhs = jnp.concatenate(
                [high[i : i + 1], high[j : j + 1], low[i : i + 1], low[j : j + 1]], axis=0
            )
            out = fold(jnp.dot(lhs.astype(BF16), linv2[i], preferred_element_type=F32))
            out = out[:, 0:K] + out[:, K:]
            tmp[pl.ds(i, 1)] = out[0:1]
            tmp[pl.ds(j, 1)] = out[1:2]
        return shuffle(tmp[...])

    def spread_out(y):
        lhs = both(y)
        w = fold(
            lax.dot_general(
                jnp.concatenate([lhs, lhs], axis=1), basis2[...],
                (((1,), (1,)), ((), ())), preferred_element_type=F32,
            )
        )
        for x in range(16):
            wt[:, x, :] = w[:, x * K : (x + 1) * K]
        return wt[...].reshape(32, K)

    def keep(ref, count, i, matrix):
        high, low = halves(matrix)
        ref[:, i * K : (i + 1) * K] = high
        ref[:, (count + i) * K : (count + i + 1) * K] = low

    def keep_down(h, matrix):
        high, low = halves(matrix)
        gs[h * K : (h + 1) * K, 0:K] = high
        gs[h * K : (h + 1) * K, K:] = low

    def put(ref, rows2, first=0):
        for i in range(rows2.shape[1] // K):
            ref[first + i] = rows2[:, i * K : (i + 1) * K]

    loads["e0"].wait()
    loads["nt0"].wait()
    p = e0[...]
    pf[0] = p
    keep(pa, 4, 3, p)
    for i in range(3):
        p = dot(p, nt[i])
        pf[i + 1] = p
        keep(pa, 4, 2 - i, p)
    loads["rs"].wait()
    for i in range(4):
        loads["basis%d" % i].wait()
        high, low = halves(basis[pl.ds(4 * i, 4)].reshape(4 * K, K))
        basis2[4 * K * i : 4 * K * (i + 1), 0:K] = high
        basis2[4 * K * i : 4 * K * (i + 1), K:] = low
    u0 = coefficients(rs)
    put(zs1, dot_w(u0, pa[...]))
    pl.semaphore_wait(barrier, len(others) + len(halo))
    send_group(zs1, zb1, 0, z_peer)

    loads["cond"].wait()
    k32 = tile_rows(cond[...])
    edges_k = send_edges(k32, krs, krb, kcs, kcb, 0)
    loads["nt1"].wait()
    r = nt[3]
    rf[0] = r
    keep(ra, 5, 4, r)
    for i in range(4):
        r = dot(r, nt[4 + i])
        rf[i + 1] = r
        keep(ra, 5, 3 - i, r)
    loads["linv"].wait()
    for i in range(16):
        high, low = halves(linv[i // 4, i % 4])
        linv2[i, :, 0:K] = high
        linv2[i, :, K:] = low
    b32 = rs[...].reshape(32, K)
    lb[...] = leaf_apply(b32)
    loads["nf"].wait()
    loads["f0"].wait()
    keep_down(0, f0[...])
    for h in range(1, 5):
        keep_down(h, dot_t(nf[h - 1], pf[h - 1]))

    wait_bytes(zb1, rsem.at[0])
    u4, u3, u2, u1 = group_sums(zs1, zb1)
    put(cs1, dot_w(u4, ra[...]))
    core1 = send(cs1, cb1, ssem.at[1], rsem.at[1], c_peer)
    for h in range(6, 8):
        keep_down(h, dot_t(dot_t(nf[h - 1], rf[h - 5]), pf[3]))
    core1.wait_recv()
    u5 = cs1[4] + cb1[4]
    gs1[...] = cs1[pl.ds(0, 4)] + cb1[pl.ds(0, 4)]
    send_group(gs1, gb1, 2, g_peer)
    for h in (5, 8, 9):
        keep_down(h, dot_t(dot_t(nf[h - 1], rf[h - 5]), pf[3]))
    y = dot_w(jnp.concatenate([u0, u1, u2, u3, u4, u5], axis=1), gs[0 : 6 * K])
    for e in edges_k:
        e.wait_recv()
    weights = [0.5 * (k32 + other) for other in beside(k32, krb, kcb)]
    wait_bytes(gb1, rsem.at[2])
    u9, u8, u7, u6 = group_sums(gs1, gb1)
    y = y + dot_w(jnp.concatenate([u6, u7, u8, u9], axis=1), gs[6 * K : 10 * K])
    z = lb[...] + spread_out(y)

    edges_z = send_edges(z, hrs, hrb, hcs, hcb, 4)
    for h in range(1, 4):
        keep(pb, 4, 3 - h, dot(pf[h - 1], nf[h - 1]))
    keep(pb, 4, 3, f0[...])
    for h in range(5, 10):
        keep(rb, 6, 9 - h, dot(rf[h - 5], nf[h - 1]))
    keep(rb, 6, 5, nf[3])
    for e in edges_z:
        e.wait_recv()
    applied = jnp.zeros_like(z)
    for weight, other in zip(weights, beside(z, hrb, hcb)):
        applied = applied + weight * (z - other)
    res_o[...] = applied.reshape(2, 16, K)

    lane2 = lane[0:2]

    def columns(t):
        return jnp.sum(t.reshape(2, 16, K), axis=1)

    def quadratic(t):
        return jnp.where(lane2 >= 64, t + pltpu.roll(t, 64, 1), 0.0)

    u0 = coefficients(res_o)
    put(zs2, dot_w(u0, pa[...]), 1)
    low = dot_w(u0, pb[...])
    put(zs2, low[:, 0 : 3 * K], 5)
    near = leaf_apply(applied)
    inner = jnp.concatenate([columns(b32 * z), columns(z * applied)], axis=0)
    inner = inner + pltpu.roll(inner, 64, 1)
    inner = inner + pltpu.roll(inner, 32, 1)
    zs2[0] = jnp.where(lane2 < 32, inner[0:2], jnp.where(lane2 < 64, inner[2:4], 0.0)) + quadratic(
        columns(applied * near) + u0 * low[:, 3 * K :]
    )
    send_all(zs2, zb2, 3, z_peer)
    wait_bytes(zb2, rsem.at[3])
    u4 = all_sums(zs2, zb2, 1, 16)[0]
    up = dot_w(u4, ra[...])
    image = dot_w(u4, rb[...])
    u3, q3 = products(zs2, zb2, 2, 5, 8)
    u2, q2 = products(zs2, zb2, 3, 6, 4)
    u1, q1 = products(zs2, zb2, 4, 7, 2)
    cs2[0] = all_sums(zs2, zb2, 0, 16)[0] + quadratic(q1 + q2 + q3 + u4 * image[:, 5 * K :])
    put(cs2, up[:, 0 : 4 * K], 1)
    put(cs2, image[:, 0 : 4 * K], 5)
    cs2[9] = up[:, 4 * K :]
    cs2[10] = image[:, 4 * K : 5 * K]
    core2 = send(cs2, cb2, ssem.at[4], rsem.at[4], c_peer)
    core2.wait_recv()
    u5 = cs2[9] + cb2[9]
    gs2[...] = cs2[pl.ds(0, 9)] + cb2[pl.ds(0, 9)]
    gs2[0] = gs2[0] + quadratic(u5 * (cs2[10] + cb2[10]))
    send_all(gs2, gb2, 5, g_peer)
    y = dot_w(jnp.concatenate([u0, u1, u2, u3, u4, u5], axis=1), gs[0 : 6 * K])
    wait_bytes(gb2, rsem.at[5])
    u9, q9 = products(gs2, gb2, 1, 5, 16)
    u8, q8 = products(gs2, gb2, 2, 6, 8)
    u7, q7 = products(gs2, gb2, 3, 7, 4)
    u6, q6 = products(gs2, gb2, 4, 8, 2)
    y = y + dot_w(jnp.concatenate([u6, u7, u8, u9], axis=1), gs[6 * K : 10 * K])
    mapped = near + spread_out(y)
    inner = all_sums(gs2, gb2, 0, 16)[0] + quadratic(q6 + q7 + q8 + q9)

    def over_lanes(t):
        return jnp.sum(t, axis=1, keepdims=True)

    rz_old = over_lanes(jnp.where(lane2 < 32, inner, 0.0))
    curvature = over_lanes(jnp.where((lane2 >= 32) & (lane2 < 64), inner, 0.0))
    squared = over_lanes(jnp.where(lane2 >= 64, inner, 0.0))
    step = rz_old / curvature
    rz_new = rz_old - 2.0 * step * curvature + step * step * squared

    def over_tile(t):
        return jnp.concatenate(
            [jnp.broadcast_to(t[0:1], (16, K)), jnp.broadcast_to(t[1:2], (16, K))], axis=0
        )

    step32 = over_tile(step)
    sol_o[...] = (step32 * z).reshape(2, 16, K)
    res_o[...] = (b32 - step32 * applied).reshape(2, 16, K)
    second = z - step32 * mapped
    dir_o[...] = (second + over_tile(rz_new / rz_old) * z).reshape(2, 16, K)

    for e in edges_k + edges_z + [core1, core2]:
        e.wait_send()
    for buf, slot in ((zb1, 0), (gb1, 2), (zb2, 3), (gb2, 5)):
        wait_bytes(buf, ssem.at[slot])


def on_device(*args):
    unit = lambda *n: pltpu.VMEM(n + (2, K), F32)
    square = lambda *n: pltpu.VMEM(n + (K, K), F32)
    out = jax.ShapeDtypeStruct((2, 16, K), F32)
    return pl.pallas_call(
        kernel,
        name="pcg_step",
        out_shape=(out, out, out),
        in_specs=[pl.BlockSpec(memory_space=pl.ANY)] * 8,
        out_specs=[pl.BlockSpec(memory_space=pltpu.VMEM)] * 3,
        scratch_shapes=[
            pltpu.VMEM((2, 16, K), F32), pltpu.VMEM((16, K), F32), square(4, 4), square(16),
            square(), square(8), square(), square(9),
            square(4), square(5), pltpu.VMEM((16 * K, 2 * K), BF16), pltpu.VMEM((16, K, 2 * K), BF16),
            pltpu.VMEM((K, 8 * K), BF16), pltpu.VMEM((K, 8 * K), BF16),
            pltpu.VMEM((K, 10 * K), BF16), pltpu.VMEM((K, 12 * K), BF16),
            pltpu.VMEM((10 * K, 2 * K), BF16),
            pltpu.VMEM((32, K), F32), pltpu.VMEM((2, 16, K), F32), pltpu.VMEM((32, K), F32),
            unit(4), unit(26), unit(8), unit(15, 8), unit(5), unit(5), unit(11), unit(11),
            unit(4), unit(26), unit(9), unit(15, 9),
            unit(2), unit(2), pltpu.VMEM((2, 8, K), F32), pltpu.VMEM((2, 8, K), F32),
            unit(2), unit(2), pltpu.VMEM((2, 8, K), F32), pltpu.VMEM((2, 8, K), F32),
            pltpu.SemaphoreType.DMA((12,)), pltpu.SemaphoreType.DMA((6,)),
            pltpu.SemaphoreType.DMA((6,)), pltpu.SemaphoreType.DMA((8,)),
            pltpu.SemaphoreType.DMA((8,)),
        ],
        compiler_params=pltpu.CompilerParams(
            collective_id=0, has_side_effects=True, vmem_limit_bytes=60 * 1024 * 1024
        ),
    )(*args)


def solution(mesh):
    return jax.shard_map(
        on_device,
        mesh=mesh,
        in_specs=(
            P(None, "gx", "gy"),
            P("gx", "gy"),
            P("gx", "gy", None, None),
            P("gx", "gy", None),
            P("gx", "gy", None, None),
            P("gx", "gy", None, None, None),
            P("gx", "gy", None, None),
            P("gx", "gy", None, None, None),
        ),
        out_specs=(P(None, "gx", "gy"), P(None, "gx", "gy"), P(None, "gx", "gy")),
        check_vma=False,
    )
```

```python
import jax
import jax.numpy as jnp
from jax import lax
from jax.experimental import pallas as pl
from jax.experimental.pallas import tpu as pltpu
from jax.sharding import PartitionSpec as P

HIGHEST = lax.Precision.HIGHEST
MESH = pl.DeviceIdType.MESH
F32 = jnp.float32
BF16 = jnp.bfloat16
K = 128


def dot(a, b):
    return lax.dot_general(
        a, b, (((1,), (0,)), ((), ())), precision=HIGHEST, preferred_element_type=F32
    )


def dot_t(a, b):
    return lax.dot_general(
        a, b, (((1,), (1,)), ((), ())), precision=HIGHEST, preferred_element_type=F32
    )


def halves(a):
    high = a.astype(BF16)
    return high, (a - high.astype(F32)).astype(BF16)


def both(a):
    return jnp.concatenate(halves(a), axis=0)


def fold(out):
    n = out.shape[0] // 2
    return out[0:n] + out[n:]


def dot_w(a, w):
    n = w.shape[1] // 2
    out = fold(jnp.dot(both(a), w, preferred_element_type=F32))
    return out[:, 0:n] + out[:, n:]


def units():
    return {d: 5 - d.bit_length() for d in range(1, 16)}


def offsets(count):
    at, out = 0, {}
    for d in sorted(count):
        out[d] = at
        at += count[d]
    return out, at


def butterfly(values):
    while len(values) > 1:
        values = [values[i] + values[i + 1] for i in range(0, len(values), 2)]
    return values[0]


ORDER = (8, 15, 14, 13, 12, 11, 10, 9, 7, 6, 5, 4, 3, 2, 1)


def tile_rows(x):
    return jnp.concatenate([x, x], axis=0)


def shuffle(t):
    row = lax.broadcasted_iota(jnp.int32, t.shape, 0) % 4
    chunk = lax.broadcasted_iota(jnp.int32, t.shape, 1) // 32
    rows, lanes = t.shape
    out = t
    for delta in (-3, -2, -1, 1, 2, 3):
        moved = pltpu.roll(t, delta % rows, 0)
        moved = pltpu.roll(moved, (-32 * delta) % lanes, 1)
        out = jnp.where(row - chunk == delta, moved, out)
    return out


def kernel(
    rs_h, cond_h, linv_h, basis_h, e0_h, nt_h, f0_h, nf_h,
    out_o,
    rs, cond, linv, basis, e0, nt, f0, nf,
    pf, rf, basis2, linv2, pa, pb, ra, rb, gs, lb, wt, tmp,
    zs1, zb1, zs2, zb2, cs1, cb1, cs2, cb2, gs1, gb1, gs2, gb2,
    hrs, hrb, hcs, hcb, krs, krb, kcs, kcb,
    lsem, ssem, rsem, hsem, hrsem,
):
    X = lax.axis_index("gx")
    Z = lax.axis_index("gy")
    z_peer = lambda d: (X, Z ^ d)
    c_peer = (X ^ 1, Z)
    g_peer = lambda d: (X ^ (2 * d), Z)
    x_up, x_down = (X + 1) % 32, (X + 31) % 32
    z_up, z_down = (Z + 1) % 16, (Z + 15) % 16

    barrier = pltpu.get_barrier_semaphore()
    others = [z_peer(d) for d in ORDER] + [g_peer(d) for d in ORDER] + [c_peer]
    others.append(((X + 31 + 2 * (X % 2)) % 32, Z))
    for who in others:
        pl.semaphore_signal(barrier, inc=1, device_id=who, device_id_type=MESH)

    loads = {}
    parts = [
        ("e0", e0_h.at[0, 0], e0),
        ("nt0", nt_h.at[0, 0, pl.ds(0, 3)], nt.at[pl.ds(0, 3)]),
        ("rs", rs_h, rs),
    ]
    for i in range(4):
        at = pl.ds(4 * i, 4)
        parts.append(("basis%d" % i, basis_h.at[at], basis.at[at]))
    parts += [
        ("nt1", nt_h.at[0, 0, pl.ds(3, 5)], nt.at[pl.ds(3, 5)]),
        ("cond", cond_h, cond),
        ("nf", nf_h.at[0, 0], nf),
        ("linv", linv_h, linv),
        ("f0", f0_h.at[0, 0], f0),
    ]
    for i, (name, src, dst) in enumerate(parts):
        loads[name] = pltpu.make_async_copy(src, dst, lsem.at[i])
        loads[name].start()

    def send(src, dst, sends, recvs, who):
        copy = pltpu.make_async_remote_copy(
            src_ref=src, dst_ref=dst, send_sem=sends, recv_sem=recvs,
            device_id=who, device_id_type=MESH,
        )
        copy.start()
        return copy

    def send_group(src, buf, slot, peer):
        count = units()
        at, _ = offsets(count)
        for d in ORDER:
            n = count[d]
            send(
                src.at[pl.ds(0, n)], buf.at[pl.ds(at[d], n)], ssem.at[slot], rsem.at[slot], peer(d)
            )

    def send_all(src, buf, slot, peer):
        for d in ORDER:
            send(src, buf.at[d - 1], ssem.at[slot], rsem.at[slot], peer(d))

    def wait_bytes(buf, sem):
        pltpu.make_async_copy(buf, buf, sem).wait()

    def group_sums(src, buf):
        count = units()
        at, _ = offsets(count)
        out = []
        for unit in range(4):
            reach = [d for d in range(1, 16) if count[d] > unit]
            out.append(butterfly([src[unit]] + [buf[at[d] + unit] for d in reach]))
        return out

    def all_sums(src, buf, unit, size):
        terms = [src[unit]] + [buf[d, unit] for d in range(15)]
        return [butterfly(terms[i : i + size]) for i in range(0, 16, size)]

    def products(src, buf, unit, other, size):
        sums = all_sums(src, buf, unit, size)
        images = all_sums(src, buf, other, size)
        return sums[0], butterfly([s * m for s, m in zip(sums, images)])

    row = lax.broadcasted_iota(jnp.int32, (32, K), 0)
    lane = lax.broadcasted_iota(jnp.int32, (32, K), 1)

    def send_edges(t, rows_src, rows_buf, cols_src, cols_buf, first):
        rows_src[0] = jnp.concatenate([t[15:16], t[31:32]], axis=0)
        rows_src[1] = jnp.concatenate([t[0:1], t[16:17]], axis=0)
        lane8 = lane[0:8]
        last_col = pltpu.roll(t[0:8], 1, 1)
        first_col = t[0:8]
        for j in range(1, 4):
            part = t[8 * j : 8 * j + 8]
            last_col = jnp.where(lane8 == j, pltpu.roll(part, j + 1, 1), last_col)
            first_col = jnp.where(lane8 == j, pltpu.roll(part, j, 1), first_col)
        cols_src[0] = last_col
        cols_src[1] = first_col
        return [
            send(rows_src.at[0], rows_buf.at[0], hsem.at[first], hrsem.at[first], (x_up, Z)),
            send(rows_src.at[1], rows_buf.at[1], hsem.at[first + 1], hrsem.at[first + 1], (x_down, Z)),
            send(cols_src.at[0], cols_buf.at[0], hsem.at[first + 2], hrsem.at[first + 2], (X, z_up)),
            send(cols_src.at[1], cols_buf.at[1], hsem.at[first + 3], hrsem.at[first + 3], (X, z_down)),
        ]

    def beside(t, rows_buf, cols_buf):
        def spread(h):
            return jnp.concatenate(
                [jnp.broadcast_to(h[0:1], (16, K)), jnp.broadcast_to(h[1:2], (16, K))], axis=0
            )

        low = spread(jnp.where(X > 0, rows_buf[0], 0.0))
        high = spread(jnp.where(X < 31, rows_buf[1], 0.0))
        left = jnp.where(Z > 0, cols_buf[0], 0.0)
        right = jnp.where(Z < 15, cols_buf[1], 0.0)
        left = jnp.concatenate([left] + [pltpu.roll(left, K - j, 1) for j in range(1, 4)], axis=0)
        right = jnp.concatenate([pltpu.roll(right, K - 1 - j, 1) for j in range(4)], axis=0)
        return (
            jnp.where(row % 16 == 15, high, pltpu.roll(t, 31, 0)),
            jnp.where(row % 16 == 0, low, pltpu.roll(t, 1, 0)),
            jnp.where(lane == K - 1, right, pltpu.roll(t, K - 1, 1)),
            jnp.where(lane == 0, left, pltpu.roll(t, 1, 1)),
        )

    def flat_rows(ref):
        return jnp.concatenate([ref[:, x, :] for x in range(16)], axis=1)

    def coefficients(ref):
        return dot_w(flat_rows(ref), basis2[...])

    def leaf_apply(t):
        high, low = halves(shuffle(t))
        high, low = high.astype(F32), low.astype(F32)
        for i in range(16):
            j = 16 + i
            lhs = jnp.concatenate(
                [high[i : i + 1], high[j : j + 1], low[i : i + 1], low[j : j + 1]], axis=0
            )
            out = fold(jnp.dot(lhs.astype(BF16), linv2[i], preferred_element_type=F32))
            out = out[:, 0:K] + out[:, K:]
            tmp[pl.ds(i, 1)] = out[0:1]
            tmp[pl.ds(j, 1)] = out[1:2]
        return shuffle(tmp[...])

    def spread_out(y):
        lhs = both(y)
        w = fold(
            lax.dot_general(
                jnp.concatenate([lhs, lhs], axis=1), basis2[...],
                (((1,), (1,)), ((), ())), preferred_element_type=F32,
            )
        )
        for x in range(16):
            wt[:, x, :] = w[:, x * K : (x + 1) * K]
        return wt[...].reshape(32, K)

    def keep(ref, count, i, matrix):
        high, low = halves(matrix)
        ref[:, i * K : (i + 1) * K] = high
        ref[:, (count + i) * K : (count + i + 1) * K] = low

    def keep_down(h, matrix):
        high, low = halves(matrix)
        gs[h * K : (h + 1) * K, 0:K] = high
        gs[h * K : (h + 1) * K, K:] = low

    def put(ref, rows2, first=0):
        for i in range(rows2.shape[1] // K):
            ref[first + i] = rows2[:, i * K : (i + 1) * K]

    loads["e0"].wait()
    loads["nt0"].wait()
    p = e0[...]
    pf[0] = p
    keep(pa, 4, 3, p)
    for i in range(3):
        p = dot(p, nt[i])
        pf[i + 1] = p
        keep(pa, 4, 2 - i, p)
    loads["rs"].wait()
    for i in range(4):
        loads["basis%d" % i].wait()
        high, low = halves(basis[pl.ds(4 * i, 4)].reshape(4 * K, K))
        basis2[4 * K * i : 4 * K * (i + 1), 0:K] = high
        basis2[4 * K * i : 4 * K * (i + 1), K:] = low
    u0 = coefficients(rs)
    put(zs1, dot_w(u0, pa[...]))
    loads["nt1"].wait()
    r = nt[3]
    rf[0] = r
    keep(ra, 5, 4, r)
    for i in range(4):
        r = dot(r, nt[4 + i])
        rf[i + 1] = r
        keep(ra, 5, 3 - i, r)
    pl.semaphore_wait(barrier, len(others))
    send_group(zs1, zb1, 0, z_peer)

    loads["cond"].wait()
    k32 = tile_rows(cond[...])
    edges_k = send_edges(k32, krs, krb, kcs, kcb, 0)
    loads["linv"].wait()
    for i in range(16):
        high, low = halves(linv[i // 4, i % 4])
        linv2[i, :, 0:K] = high
        linv2[i, :, K:] = low
    b32 = rs[...].reshape(32, K)
    lb[...] = leaf_apply(b32)
    loads["nf"].wait()
    loads["f0"].wait()
    keep_down(0, f0[...])
    for h in range(1, 5):
        keep_down(h, dot_t(nf[h - 1], pf[h - 1]))
    for h in range(5, 10):
        keep_down(h, dot_t(dot_t(nf[h - 1], rf[h - 5]), pf[3]))

    wait_bytes(zb1, rsem.at[0])
    u4, u3, u2, u1 = group_sums(zs1, zb1)
    put(cs1, dot_w(u4, ra[...]))
    core1 = send(cs1, cb1, ssem.at[1], rsem.at[1], c_peer)
    core1.wait_recv()
    u5 = cs1[4] + cb1[4]
    gs1[...] = cs1[pl.ds(0, 4)] + cb1[pl.ds(0, 4)]
    send_group(gs1, gb1, 2, g_peer)
    for h in range(1, 4):
        keep(pb, 4, 3 - h, dot(pf[h - 1], nf[h - 1]))
    keep(pb, 4, 3, f0[...])
    for h in range(5, 10):
        keep(rb, 6, 9 - h, dot(rf[h - 5], nf[h - 1]))
    keep(rb, 6, 5, nf[3])
    y = dot_w(jnp.concatenate([u0, u1, u2, u3, u4, u5], axis=1), gs[0 : 6 * K])
    for e in edges_k:
        e.wait_recv()
    weights = [0.5 * (k32 + other) for other in beside(k32, krb, kcb)]
    wait_bytes(gb1, rsem.at[2])
    u9, u8, u7, u6 = group_sums(gs1, gb1)
    y = y + dot_w(jnp.concatenate([u6, u7, u8, u9], axis=1), gs[6 * K : 10 * K])
    z = lb[...] + spread_out(y)

    edges_z = send_edges(z, hrs, hrb, hcs, hcb, 4)
    for e in edges_z:
        e.wait_recv()
    applied = jnp.zeros_like(z)
    for weight, other in zip(weights, beside(z, hrb, hcb)):
        applied = applied + weight * (z - other)
    wt[...] = applied.reshape(2, 16, K)

    lane2 = lane[0:2]

    def columns(t):
        return jnp.sum(t.reshape(2, 16, K), axis=1)

    def quadratic(t):
        return jnp.where(lane2 >= 64, t + pltpu.roll(t, 64, 1), 0.0)

    u0 = coefficients(wt)
    put(zs2, dot_w(u0, pa[...]), 1)
    low = dot_w(u0, pb[...])
    put(zs2, low[:, 0 : 3 * K], 5)
    near = leaf_apply(applied)
    inner = jnp.concatenate([columns(b32 * z), columns(z * applied)], axis=0)
    inner = inner + pltpu.roll(inner, 64, 1)
    inner = inner + pltpu.roll(inner, 32, 1)
    zs2[0] = jnp.where(lane2 < 32, inner[0:2], jnp.where(lane2 < 64, inner[2:4], 0.0)) + quadratic(
        columns(applied * near) + u0 * low[:, 3 * K :]
    )
    send_all(zs2, zb2, 3, z_peer)
    wait_bytes(zb2, rsem.at[3])
    u4 = all_sums(zs2, zb2, 1, 16)[0]
    up = dot_w(u4, ra[...])
    image = dot_w(u4, rb[...])
    u3, q3 = products(zs2, zb2, 2, 5, 8)
    u2, q2 = products(zs2, zb2, 3, 6, 4)
    u1, q1 = products(zs2, zb2, 4, 7, 2)
    cs2[0] = all_sums(zs2, zb2, 0, 16)[0] + quadratic(q1 + q2 + q3 + u4 * image[:, 5 * K :])
    put(cs2, up[:, 0 : 4 * K], 1)
    put(cs2, image[:, 0 : 4 * K], 5)
    cs2[9] = up[:, 4 * K :]
    cs2[10] = image[:, 4 * K : 5 * K]
    core2 = send(cs2, cb2, ssem.at[4], rsem.at[4], c_peer)
    core2.wait_recv()
    u5 = cs2[9] + cb2[9]
    gs2[...] = cs2[pl.ds(0, 9)] + cb2[pl.ds(0, 9)]
    gs2[0] = gs2[0] + quadratic(u5 * (cs2[10] + cb2[10]))
    send_all(gs2, gb2, 5, g_peer)
    y = dot_w(jnp.concatenate([u0, u1, u2, u3, u4, u5], axis=1), gs[0 : 6 * K])
    wait_bytes(gb2, rsem.at[5])
    u9, q9 = products(gs2, gb2, 1, 5, 16)
    u8, q8 = products(gs2, gb2, 2, 6, 8)
    u7, q7 = products(gs2, gb2, 3, 7, 4)
    u6, q6 = products(gs2, gb2, 4, 8, 2)
    y = y + dot_w(jnp.concatenate([u6, u7, u8, u9], axis=1), gs[6 * K : 10 * K])
    mapped = near + spread_out(y)
    inner = all_sums(gs2, gb2, 0, 16)[0] + quadratic(q6 + q7 + q8 + q9)

    def over_lanes(t):
        return jnp.sum(t, axis=1, keepdims=True)

    rz_old = over_lanes(jnp.where(lane2 < 32, inner, 0.0))
    curvature = over_lanes(jnp.where((lane2 >= 32) & (lane2 < 64), inner, 0.0))
    squared = over_lanes(jnp.where(lane2 >= 64, inner, 0.0))
    step = rz_old / curvature
    rz_new = rz_old - 2.0 * step * curvature + step * step * squared

    def over_tile(t):
        return jnp.concatenate(
            [jnp.broadcast_to(t[0:1], (16, K)), jnp.broadcast_to(t[1:2], (16, K))], axis=0
        )

    step32 = over_tile(step)
    out_o[0:2] = (step32 * z).reshape(2, 16, K)
    out_o[2:4] = (b32 - step32 * applied).reshape(2, 16, K)
    second = z - step32 * mapped
    out_o[4:6] = (second + over_tile(rz_new / rz_old) * z).reshape(2, 16, K)

    for e in edges_k + edges_z + [core1, core2]:
        e.wait_send()
    for buf, slot in ((zb1, 0), (gb1, 2), (zb2, 3), (gb2, 5)):
        wait_bytes(buf, ssem.at[slot])


def on_device(*args):
    unit = lambda *n: pltpu.VMEM(n + (2, K), F32)
    square = lambda *n: pltpu.VMEM(n + (K, K), F32)
    out = pl.pallas_call(
        kernel,
        name="pcg_step",
        out_shape=jax.ShapeDtypeStruct((6, 16, K), F32),
        in_specs=[pl.BlockSpec(memory_space=pl.ANY)] * 8,
        out_specs=pl.BlockSpec(memory_space=pltpu.VMEM),
        scratch_shapes=[
            pltpu.VMEM((2, 16, K), F32), pltpu.VMEM((16, K), F32), square(4, 4), square(16),
            square(), square(8), square(), square(9),
            square(4), square(5), pltpu.VMEM((16 * K, 2 * K), BF16), pltpu.VMEM((16, K, 2 * K), BF16),
            pltpu.VMEM((K, 8 * K), BF16), pltpu.VMEM((K, 8 * K), BF16),
            pltpu.VMEM((K, 10 * K), BF16), pltpu.VMEM((K, 12 * K), BF16),
            pltpu.VMEM((10 * K, 2 * K), BF16),
            pltpu.VMEM((32, K), F32), pltpu.VMEM((2, 16, K), F32), pltpu.VMEM((32, K), F32),
            unit(4), unit(26), unit(8), unit(15, 8), unit(5), unit(5), unit(11), unit(11),
            unit(4), unit(26), unit(9), unit(15, 9),
            unit(2), unit(2), pltpu.VMEM((2, 8, K), F32), pltpu.VMEM((2, 8, K), F32),
            unit(2), unit(2), pltpu.VMEM((2, 8, K), F32), pltpu.VMEM((2, 8, K), F32),
            pltpu.SemaphoreType.DMA((12,)), pltpu.SemaphoreType.DMA((6,)),
            pltpu.SemaphoreType.DMA((6,)), pltpu.SemaphoreType.DMA((8,)),
            pltpu.SemaphoreType.DMA((8,)),
        ],
        compiler_params=pltpu.CompilerParams(
            collective_id=0, has_side_effects=True, vmem_limit_bytes=60 * 1024 * 1024
        ),
    )(*args)
    return out[0:2], out[2:4], out[4:6]


def solution(mesh):
    return jax.shard_map(
        on_device,
        mesh=mesh,
        in_specs=(
            P(None, "gx", "gy"),
            P("gx", "gy"),
            P("gx", "gy", None, None),
            P("gx", "gy", None),
            P("gx", "gy", None, None),
            P("gx", "gy", None, None, None),
            P("gx", "gy", None, None),
            P("gx", "gy", None, None, None),
        ),
        out_specs=(P(None, "gx", "gy"), P(None, "gx", "gy"), P(None, "gx", "gy")),
        check_vma=False,
    )
```

```python
import jax
import jax.numpy as jnp
from jax import lax
from jax.experimental import pallas as pl
from jax.experimental.pallas import tpu as pltpu
from jax.sharding import PartitionSpec as P

HIGHEST = lax.Precision.HIGHEST
MESH = pl.DeviceIdType.MESH
F32 = jnp.float32
BF16 = jnp.bfloat16
K = 128


def dot(a, b):
    return lax.dot_general(
        a, b, (((1,), (0,)), ((), ())), precision=HIGHEST, preferred_element_type=F32
    )


def dot_t(a, b):
    return lax.dot_general(
        a, b, (((1,), (1,)), ((), ())), precision=HIGHEST, preferred_element_type=F32
    )


def halves(a):
    high = a.astype(BF16)
    return high, (a - high.astype(F32)).astype(BF16)


def both(a):
    return jnp.concatenate(halves(a), axis=0)


def fold(out):
    n = out.shape[0] // 2
    return out[0:n] + out[n:]


def dot_w(a, w):
    n = w.shape[1] // 2
    out = fold(jnp.dot(both(a), w, preferred_element_type=F32))
    return out[:, 0:n] + out[:, n:]


def units():
    return {d: 5 - d.bit_length() for d in range(1, 16)}


def offsets(count):
    at, out = 0, {}
    for d in sorted(count):
        out[d] = at
        at += count[d]
    return out, at


def butterfly(values):
    while len(values) > 1:
        values = [values[i] + values[i + 1] for i in range(0, len(values), 2)]
    return values[0]


ORDER = (8, 15, 14, 13, 12, 11, 10, 9, 7, 6, 5, 4, 3, 2, 1)


def tile_rows(x):
    return jnp.concatenate([x, x], axis=0)


def shuffle(t):
    row = lax.broadcasted_iota(jnp.int32, t.shape, 0) % 4
    chunk = lax.broadcasted_iota(jnp.int32, t.shape, 1) // 32
    rows, lanes = t.shape
    out = t
    for delta in (-3, -2, -1, 1, 2, 3):
        moved = pltpu.roll(t, delta % rows, 0)
        moved = pltpu.roll(moved, (-32 * delta) % lanes, 1)
        out = jnp.where(row - chunk == delta, moved, out)
    return out


def kernel(
    rs_h, cond_h, linv_h, basis_h, e0_h, nt_h, f0_h, nf_h,
    out_o,
    rs, cond, linv, basis, e0, nt, f0, nf,
    pf, rf, basis2, linv2, pa, pb, ra, rb, gs, lb, wt, tmp,
    zs1, zb1, zs2, zb2, cs1, cb1, cs2, cb2, gs1, gb1, gs2, gb2,
    hrs, hrb, hcs, hcb, krs, krb, kcs, kcb,
    hxs, hxb, hx2, hzs, hzb, hz2,
    lsem, ssem, rsem, hsem, hrsem, msem, mrsem,
):
    X = lax.axis_index("gx")
    Z = lax.axis_index("gy")
    z_peer = lambda d: (X, Z ^ d)
    c_peer = (X ^ 1, Z)
    g_peer = lambda d: (X ^ (2 * d), Z)
    even = X % 2 == 0
    beyond = (X + 31 + 2 * (X % 2)) % 32
    z_up, z_down = (Z + 1) % 16, (Z + 15) % 16

    barrier = pltpu.get_barrier_semaphore()
    others = [z_peer(d) for d in ORDER] + [g_peer(d) for d in ORDER] + [c_peer]
    others.append((beyond, Z))
    for who in others:
        pl.semaphore_signal(barrier, inc=1, device_id=who, device_id_type=MESH)

    loads = {}
    parts = [
        ("e0", e0_h.at[0, 0], e0),
        ("nt0", nt_h.at[0, 0, pl.ds(0, 3)], nt.at[pl.ds(0, 3)]),
        ("rs", rs_h, rs),
    ]
    for i in range(4):
        at = pl.ds(4 * i, 4)
        parts.append(("basis%d" % i, basis_h.at[at], basis.at[at]))
    parts += [
        ("nt1", nt_h.at[0, 0, pl.ds(3, 5)], nt.at[pl.ds(3, 5)]),
        ("cond", cond_h, cond),
        ("nf", nf_h.at[0, 0], nf),
        ("linv", linv_h, linv),
        ("f0", f0_h.at[0, 0], f0),
    ]
    for i, (name, src, dst) in enumerate(parts):
        loads[name] = pltpu.make_async_copy(src, dst, lsem.at[i])
        loads[name].start()

    def send(src, dst, sends, recvs, who):
        copy = pltpu.make_async_remote_copy(
            src_ref=src, dst_ref=dst, send_sem=sends, recv_sem=recvs,
            device_id=who, device_id_type=MESH,
        )
        copy.start()
        return copy

    def send_group(src, buf, slot, peer):
        count = units()
        at, _ = offsets(count)
        for d in ORDER:
            n = count[d]
            send(
                src.at[pl.ds(0, n)], buf.at[pl.ds(at[d], n)], ssem.at[slot], rsem.at[slot], peer(d)
            )

    def send_all(src, buf, slot, peer):
        for d in ORDER:
            send(src, buf.at[d - 1], ssem.at[slot], rsem.at[slot], peer(d))

    def wait_bytes(buf, sem):
        pltpu.make_async_copy(buf, buf, sem).wait()

    def group_sums(src, buf):
        count = units()
        at, _ = offsets(count)
        out = []
        for unit in range(4):
            reach = [d for d in range(1, 16) if count[d] > unit]
            out.append(butterfly([src[unit]] + [buf[at[d] + unit] for d in reach]))
        return out

    def all_sums(src, buf, unit, size):
        terms = [src[unit]] + [buf[d, unit] for d in range(15)]
        return [butterfly(terms[i : i + size]) for i in range(0, 16, size)]

    def products(src, buf, unit, other, size):
        sums = all_sums(src, buf, unit, size)
        images = all_sums(src, buf, other, size)
        return sums[0], butterfly([s * m for s, m in zip(sums, images)])

    row = lax.broadcasted_iota(jnp.int32, (32, K), 0)
    lane = lax.broadcasted_iota(jnp.int32, (32, K), 1)

    def send_edges(t, rows_src, rows_buf, cols_src, cols_buf, first):
        first_row = jnp.concatenate([t[0:1], t[16:17]], axis=0)
        last_row = jnp.concatenate([t[15:16], t[31:32]], axis=0)
        rows_src[0] = jnp.where(even, last_row, first_row)
        rows_src[1] = jnp.where(even, first_row, last_row)
        lane8 = lane[0:8]
        last_col = pltpu.roll(t[0:8], 1, 1)
        first_col = t[0:8]
        for j in range(1, 4):
            part = t[8 * j : 8 * j + 8]
            last_col = jnp.where(lane8 == j, pltpu.roll(part, j + 1, 1), last_col)
            first_col = jnp.where(lane8 == j, pltpu.roll(part, j, 1), first_col)
        cols_src[0] = last_col
        cols_src[1] = first_col
        return [
            send(rows_src.at[0], rows_buf.at[0], hsem.at[first], hrsem.at[first], c_peer),
            send(rows_src.at[1], rows_buf.at[1], hsem.at[first + 1], hrsem.at[first + 1], (beyond, Z)),
            send(cols_src.at[0], cols_buf.at[0], hsem.at[first + 2], hrsem.at[first + 2], (X, z_up)),
            send(cols_src.at[1], cols_buf.at[1], hsem.at[first + 3], hrsem.at[first + 3], (X, z_down)),
        ]

    def beside(t, rows_buf, cols_buf, late=None):
        def spread(h):
            return jnp.concatenate(
                [jnp.broadcast_to(h[0:1], (16, K)), jnp.broadcast_to(h[1:2], (16, K))], axis=0
            )

        inside, outside = rows_buf[0], rows_buf[1]
        if late is not None:
            inside, outside = inside + late[0], outside + late[1]
        low = spread(jnp.where(X > 0, jnp.where(even, outside, inside), 0.0))
        high = spread(jnp.where(X < 31, jnp.where(even, inside, outside), 0.0))
        left, right = cols_buf[0], cols_buf[1]
        left = jnp.concatenate([left] + [pltpu.roll(left, K - j, 1) for j in range(1, 4)], axis=0)
        right = jnp.concatenate([pltpu.roll(right, K - 1 - j, 1) for j in range(4)], axis=0)
        if late is not None:
            left, right = left + late[2], right + late[3]
        left = jnp.where(Z > 0, left, 0.0)
        right = jnp.where(Z < 15, right, 0.0)
        return (
            jnp.where(row % 16 == 15, high, pltpu.roll(t, 31, 0)),
            jnp.where(row % 16 == 0, low, pltpu.roll(t, 1, 0)),
            jnp.where(lane == K - 1, right, pltpu.roll(t, K - 1, 1)),
            jnp.where(lane == 0, left, pltpu.roll(t, 1, 1)),
        )

    def flat_rows(ref):
        return jnp.concatenate([ref[:, x, :] for x in range(16)], axis=1)

    def coefficients(ref):
        return dot_w(flat_rows(ref), basis2[...])

    def leaf_apply(t):
        high, low = halves(shuffle(t))
        high, low = high.astype(F32), low.astype(F32)
        for i in range(16):
            j = 16 + i
            lhs = jnp.concatenate(
                [high[i : i + 1], high[j : j + 1], low[i : i + 1], low[j : j + 1]], axis=0
            )
            out = fold(jnp.dot(lhs.astype(BF16), linv2[i], preferred_element_type=F32))
            out = out[:, 0:K] + out[:, K:]
            tmp[pl.ds(i, 1)] = out[0:1]
            tmp[pl.ds(j, 1)] = out[1:2]
        return shuffle(tmp[...])

    def spread_out(y):
        lhs = both(y)
        w = fold(
            lax.dot_general(
                jnp.concatenate([lhs, lhs], axis=1), basis2[...],
                (((1,), (1,)), ((), ())), preferred_element_type=F32,
            )
        )
        for x in range(16):
            wt[:, x, :] = w[:, x * K : (x + 1) * K]
        return wt[...].reshape(32, K)

    def keep(ref, count, i, matrix):
        high, low = halves(matrix)
        ref[:, i * K : (i + 1) * K] = high
        ref[:, (count + i) * K : (count + i + 1) * K] = low

    def keep_down(h, matrix):
        high, low = halves(matrix)
        gs[h * K : (h + 1) * K, 0:K] = high
        gs[h * K : (h + 1) * K, K:] = low

    def put(ref, rows2, first=0):
        for i in range(rows2.shape[1] // K):
            ref[first + i] = rows2[:, i * K : (i + 1) * K]

    loads["e0"].wait()
    loads["nt0"].wait()
    p = e0[...]
    pf[0] = p
    keep(pa, 4, 3, p)
    for i in range(3):
        p = dot(p, nt[i])
        pf[i + 1] = p
        keep(pa, 4, 2 - i, p)
    loads["rs"].wait()
    for i in range(4):
        loads["basis%d" % i].wait()
        high, low = halves(basis[pl.ds(4 * i, 4)].reshape(4 * K, K))
        basis2[4 * K * i : 4 * K * (i + 1), 0:K] = high
        basis2[4 * K * i : 4 * K * (i + 1), K:] = low
    u0 = coefficients(rs)
    put(zs1, dot_w(u0, pa[...]))
    loads["nt1"].wait()
    r = nt[3]
    rf[0] = r
    keep(ra, 5, 4, r)
    for i in range(4):
        r = dot(r, nt[4 + i])
        rf[i + 1] = r
        keep(ra, 5, 3 - i, r)
    loads["nf"].wait()

    def image(h):
        return dot_t(dot_t(nf[h - 1], rf[h - 5]), pf[3])

    images = {h: image(h) for h in (6, 7, 8)}
    pl.semaphore_wait(barrier, len(others))
    send_group(zs1, zb1, 0, z_peer)

    images[9] = image(9)
    edge_rows = jnp.concatenate(
        [jnp.where(even, basis[15], basis[0]), jnp.where(even, basis[0], basis[15])], axis=0
    )
    edge_cols = jnp.concatenate([basis[:, K - 1, :], basis[:, 0, :]], axis=0)
    for h in range(6, 10):
        at = (h - 6) * K
        keep_down(h, images[h])
        of_rows = dot_t(images[h], edge_rows)
        hxs[0, at : at + K] = of_rows[:, 0:K]
        hxs[1, at : at + K] = of_rows[:, K:]
        of_cols = dot_t(edge_cols, images[h])
        hzs[0, :, at : at + K] = of_cols[0:16]
        hzs[1, :, at : at + K] = of_cols[16:]
    matrices = [
        send(hxs.at[0], hxb.at[0], msem.at[0], mrsem.at[0], c_peer),
        send(hxs.at[1], hxb.at[1], msem.at[1], mrsem.at[1], (beyond, Z)),
        send(hzs.at[0], hzb.at[0], msem.at[2], mrsem.at[2], (X, z_up)),
        send(hzs.at[1], hzb.at[1], msem.at[3], mrsem.at[3], (X, z_down)),
    ]
    loads["cond"].wait()
    k32 = tile_rows(cond[...])
    edges_k = send_edges(k32, krs, krb, kcs, kcb, 0)
    loads["linv"].wait()
    for i in range(16):
        high, low = halves(linv[i // 4, i % 4])
        linv2[i, :, 0:K] = high
        linv2[i, :, K:] = low
    b32 = rs[...].reshape(32, K)
    lb[...] = leaf_apply(b32)
    loads["f0"].wait()
    keep_down(0, f0[...])
    for h in range(1, 5):
        keep_down(h, dot_t(nf[h - 1], pf[h - 1]))
    keep_down(5, image(5))

    wait_bytes(zb1, rsem.at[0])
    u4, u3, u2, u1 = group_sums(zs1, zb1)
    put(cs1, dot_w(u4, ra[...]))
    core1 = send(cs1, cb1, ssem.at[1], rsem.at[1], c_peer)
    core1.wait_recv()
    u5 = cs1[4] + cb1[4]
    gs1[...] = cs1[pl.ds(0, 4)] + cb1[pl.ds(0, 4)]
    send_all(gs1, gb1, 2, g_peer)
    y = dot_w(jnp.concatenate([u0, u1, u2, u3, u4, u5], axis=1), gs[0 : 6 * K])
    z = lb[...] + spread_out(y)
    edges_z = send_edges(z, hrs, hrb, hcs, hcb, 4)
    for h in range(1, 4):
        keep(pb, 4, 3 - h, dot(pf[h - 1], nf[h - 1]))
    keep(pb, 4, 3, f0[...])
    for h in range(5, 10):
        keep(rb, 6, 9 - h, dot(rf[h - 5], nf[h - 1]))
    keep(rb, 6, 5, nf[3])
    for e in edges_k:
        e.wait_recv()
    weights = [0.5 * (k32 + other) for other in beside(k32, krb, kcb)]
    for m in matrices:
        m.wait_recv()
    for side in range(2):
        high, low = halves(hxb[side])
        hx2[side, :, 0:K] = high
        hx2[side, :, K:] = low
        high, low = halves(hzb[side])
        hz2[16 * side : 16 * side + 16] = high
        hz2[32 + 16 * side : 48 + 16 * side] = low
    for e in edges_z:
        e.wait_recv()
    wait_bytes(gb1, rsem.at[2])
    u9 = all_sums(gs1, gb1, 0, 16)[0]
    all8, all7, all6 = [all_sums(gs1, gb1, 4 - n, 2**n) for n in (3, 2, 1)]
    mine = jnp.concatenate([all6[0], all7[0], all8[0], u9], axis=1)
    apart = (X // 2) ^ (beyond // 2)
    theirs6 = jnp.where(
        apart == 15, all6[7], jnp.where(apart == 7, all6[3], jnp.where(apart == 3, all6[1], all6[0]))
    )
    theirs7 = jnp.where(apart == 15, all7[3], jnp.where(apart == 7, all7[1], all7[0]))
    theirs8 = jnp.where(apart == 15, all8[1], all8[0])
    theirs = jnp.concatenate([theirs6, theirs7, theirs8, u9], axis=1)
    z = z + spread_out(dot_w(mine, gs[6 * K : 10 * K]))
    cols = fold(
        lax.dot_general(
            hz2[...], both(mine), (((1,), (1,)), ((), ())), preferred_element_type=F32
        )
    )
    cols = cols[:, 0:2] + cols[:, 2:4]

    def column(side):
        part = cols[16 * side : 16 * side + 16]
        return jnp.concatenate(
            [jnp.broadcast_to(part[:, i : i + 1], (16, K)) for i in range(2)], axis=0
        )

    late = (dot_w(mine, hx2[0]), dot_w(theirs, hx2[1]), column(0), column(1))
    applied = jnp.zeros_like(z)
    for weight, other in zip(weights, beside(z, hrb, hcb, late)):
        applied = applied + weight * (z - other)
    wt[...] = applied.reshape(2, 16, K)

    lane2 = lane[0:2]

    def columns(t):
        return jnp.sum(t.reshape(2, 16, K), axis=1)

    def quadratic(t):
        return jnp.where(lane2 >= 64, t + pltpu.roll(t, 64, 1), 0.0)

    u0 = coefficients(wt)
    put(zs2, dot_w(u0, pa[...]), 1)
    low = dot_w(u0, pb[...])
    put(zs2, low[:, 0 : 3 * K], 5)
    near = leaf_apply(applied)
    inner = jnp.concatenate([columns(b32 * z), columns(z * applied)], axis=0)
    inner = inner + pltpu.roll(inner, 64, 1)
    inner = inner + pltpu.roll(inner, 32, 1)
    zs2[0] = jnp.where(lane2 < 32, inner[0:2], jnp.where(lane2 < 64, inner[2:4], 0.0)) + quadratic(
        columns(applied * near) + u0 * low[:, 3 * K :]
    )
    send_all(zs2, zb2, 3, z_peer)
    wait_bytes(zb2, rsem.at[3])
    u4 = all_sums(zs2, zb2, 1, 16)[0]
    up = dot_w(u4, ra[...])
    mapped_up = dot_w(u4, rb[...])
    u3, q3 = products(zs2, zb2, 2, 5, 8)
    u2, q2 = products(zs2, zb2, 3, 6, 4)
    u1, q1 = products(zs2, zb2, 4, 7, 2)
    cs2[0] = all_sums(zs2, zb2, 0, 16)[0] + quadratic(q1 + q2 + q3 + u4 * mapped_up[:, 5 * K :])
    put(cs2, up[:, 0 : 4 * K], 1)
    put(cs2, mapped_up[:, 0 : 4 * K], 5)
    cs2[9] = up[:, 4 * K :]
    cs2[10] = mapped_up[:, 4 * K : 5 * K]
    core2 = send(cs2, cb2, ssem.at[4], rsem.at[4], c_peer)
    core2.wait_recv()
    u5 = cs2[9] + cb2[9]
    gs2[...] = cs2[pl.ds(0, 9)] + cb2[pl.ds(0, 9)]
    gs2[0] = gs2[0] + quadratic(u5 * (cs2[10] + cb2[10]))
    send_all(gs2, gb2, 5, g_peer)
    y = dot_w(jnp.concatenate([u0, u1, u2, u3, u4, u5], axis=1), gs[0 : 6 * K])
    wait_bytes(gb2, rsem.at[5])
    u9, q9 = products(gs2, gb2, 1, 5, 16)
    u8, q8 = products(gs2, gb2, 2, 6, 8)
    u7, q7 = products(gs2, gb2, 3, 7, 4)
    u6, q6 = products(gs2, gb2, 4, 8, 2)
    y = y + dot_w(jnp.concatenate([u6, u7, u8, u9], axis=1), gs[6 * K : 10 * K])
    mapped = near + spread_out(y)
    inner = all_sums(gs2, gb2, 0, 16)[0] + quadratic(q6 + q7 + q8 + q9)

    def over_lanes(t):
        return jnp.sum(t, axis=1, keepdims=True)

    rz_old = over_lanes(jnp.where(lane2 < 32, inner, 0.0))
    curvature = over_lanes(jnp.where((lane2 >= 32) & (lane2 < 64), inner, 0.0))
    squared = over_lanes(jnp.where(lane2 >= 64, inner, 0.0))
    step = rz_old / curvature
    rz_new = rz_old - 2.0 * step * curvature + step * step * squared

    def over_tile(t):
        return jnp.concatenate(
            [jnp.broadcast_to(t[0:1], (16, K)), jnp.broadcast_to(t[1:2], (16, K))], axis=0
        )

    step32 = over_tile(step)
    out_o[0:2] = (step32 * z).reshape(2, 16, K)
    out_o[2:4] = (b32 - step32 * applied).reshape(2, 16, K)
    second = z - step32 * mapped
    out_o[4:6] = (second + over_tile(rz_new / rz_old) * z).reshape(2, 16, K)

    for e in edges_k + edges_z + matrices + [core1, core2]:
        e.wait_send()
    for buf, slot in ((zb1, 0), (gb1, 2), (zb2, 3), (gb2, 5)):
        wait_bytes(buf, ssem.at[slot])


def on_device(*args):
    unit = lambda *n: pltpu.VMEM(n + (2, K), F32)
    square = lambda *n: pltpu.VMEM(n + (K, K), F32)
    out = pl.pallas_call(
        kernel,
        name="pcg_step",
        out_shape=jax.ShapeDtypeStruct((6, 16, K), F32),
        in_specs=[pl.BlockSpec(memory_space=pl.ANY)] * 8,
        out_specs=pl.BlockSpec(memory_space=pltpu.VMEM),
        scratch_shapes=[
            pltpu.VMEM((2, 16, K), F32), pltpu.VMEM((16, K), F32), square(4, 4), square(16),
            square(), square(8), square(), square(9),
            square(4), square(5), pltpu.VMEM((16 * K, 2 * K), BF16), pltpu.VMEM((16, K, 2 * K), BF16),
            pltpu.VMEM((K, 8 * K), BF16), pltpu.VMEM((K, 8 * K), BF16),
            pltpu.VMEM((K, 10 * K), BF16), pltpu.VMEM((K, 12 * K), BF16),
            pltpu.VMEM((10 * K, 2 * K), BF16),
            pltpu.VMEM((32, K), F32), pltpu.VMEM((2, 16, K), F32), pltpu.VMEM((32, K), F32),
            unit(4), unit(26), unit(8), unit(15, 8), unit(5), unit(5), unit(11), unit(11),
            unit(4), unit(15, 4), unit(9), unit(15, 9),
            unit(2), unit(2), pltpu.VMEM((2, 8, K), F32), pltpu.VMEM((2, 8, K), F32),
            unit(2), unit(2), pltpu.VMEM((2, 8, K), F32), pltpu.VMEM((2, 8, K), F32),
            pltpu.VMEM((2, 4 * K, K), F32), pltpu.VMEM((2, 4 * K, K), F32),
            pltpu.VMEM((2, 4 * K, 2 * K), BF16),
            pltpu.VMEM((2, 16, 4 * K), F32), pltpu.VMEM((2, 16, 4 * K), F32),
            pltpu.VMEM((64, 4 * K), BF16),
            pltpu.SemaphoreType.DMA((12,)), pltpu.SemaphoreType.DMA((6,)),
            pltpu.SemaphoreType.DMA((6,)), pltpu.SemaphoreType.DMA((8,)),
            pltpu.SemaphoreType.DMA((8,)), pltpu.SemaphoreType.DMA((4,)),
            pltpu.SemaphoreType.DMA((4,)),
        ],
        compiler_params=pltpu.CompilerParams(
            collective_id=0, has_side_effects=True, vmem_limit_bytes=60 * 1024 * 1024
        ),
    )(*args)
    return out[0:2], out[2:4], out[4:6]


def solution(mesh):
    return jax.shard_map(
        on_device,
        mesh=mesh,
        in_specs=(
            P(None, "gx", "gy"),
            P("gx", "gy"),
            P("gx", "gy", None, None),
            P("gx", "gy", None),
            P("gx", "gy", None, None),
            P("gx", "gy", None, None, None),
            P("gx", "gy", None, None),
            P("gx", "gy", None, None, None),
        ),
        out_specs=(P(None, "gx", "gy"), P(None, "gx", "gy"), P(None, "gx", "gy")),
        check_vma=False,
    )
```

```python
import jax
import jax.numpy as jnp
from jax import lax
from jax.experimental import pallas as pl
from jax.experimental.pallas import tpu as pltpu
from jax.sharding import PartitionSpec as P

HIGHEST = lax.Precision.HIGHEST
MESH = pl.DeviceIdType.MESH
F32 = jnp.float32
BF16 = jnp.bfloat16
K = 128


def dot(a, b):
    return lax.dot_general(
        a, b, (((1,), (0,)), ((), ())), precision=HIGHEST, preferred_element_type=F32
    )


def dot_t(a, b):
    return lax.dot_general(
        a, b, (((1,), (1,)), ((), ())), precision=HIGHEST, preferred_element_type=F32
    )


def halves(a):
    high = a.astype(BF16)
    return high, (a - high.astype(F32)).astype(BF16)


def both(a):
    return jnp.concatenate(halves(a), axis=0)


def fold(out):
    n = out.shape[0] // 2
    return out[0:n] + out[n:]


def dot_w(a, w):
    n = w.shape[1] // 2
    out = fold(jnp.dot(both(a), w, preferred_element_type=F32))
    return out[:, 0:n] + out[:, n:]


def units():
    return {d: 5 - d.bit_length() for d in range(1, 16)}


def offsets(count):
    at, out = 0, {}
    for d in sorted(count):
        out[d] = at
        at += count[d]
    return out, at


def butterfly(values):
    while len(values) > 1:
        values = [values[i] + values[i + 1] for i in range(0, len(values), 2)]
    return values[0]


ORDER = (8, 15, 14, 13, 12, 11, 10, 9, 7, 6, 5, 4, 3, 2, 1)


def tile_rows(x):
    return jnp.concatenate([x, x], axis=0)


def shuffle(t):
    row = lax.broadcasted_iota(jnp.int32, t.shape, 0) % 4
    chunk = lax.broadcasted_iota(jnp.int32, t.shape, 1) // 32
    rows, lanes = t.shape
    out = t
    for delta in (-3, -2, -1, 1, 2, 3):
        moved = pltpu.roll(t, delta % rows, 0)
        moved = pltpu.roll(moved, (-32 * delta) % lanes, 1)
        out = jnp.where(row - chunk == delta, moved, out)
    return out


def kernel(
    rs_h, cond_h, linv_h, basis_h, e0_h, nt_h, f0_h, nf_h,
    out_o,
    rs, cond, linv, basis, e0, nt, f0, nf,
    pf, rf, basis2, linv2, pa, pb, ra, rb, gs, lb, wt, tmp,
    zs1, zb1, zs2, zb2, cs1, cb1, cs2, cb2, gs1, gb1, gs2, gb2,
    hrs, hrb, hcs, hcb, krs, krb, kcs, kcb,
    hxs, hxb, hx2, hzs, hzb, hz2, out,
    lsem, ssem, rsem, hsem, hrsem, msem, mrsem,
):
    X = lax.axis_index("gx")
    Z = lax.axis_index("gy")
    z_peer = lambda d: (X, Z ^ d)
    c_peer = (X ^ 1, Z)
    g_peer = lambda d: (X ^ (2 * d), Z)
    even = X % 2 == 0
    beyond = (X + 31 + 2 * (X % 2)) % 32
    z_up, z_down = (Z + 1) % 16, (Z + 15) % 16

    barrier = pltpu.get_barrier_semaphore()
    others = [z_peer(d) for d in ORDER] + [g_peer(d) for d in ORDER] + [c_peer]
    others.append((beyond, Z))
    for who in others:
        pl.semaphore_signal(barrier, inc=1, device_id=who, device_id_type=MESH)

    loads = {}
    parts = [
        ("e0", e0_h.at[0, 0], e0),
        ("nt0", nt_h.at[0, 0, pl.ds(0, 3)], nt.at[pl.ds(0, 3)]),
        ("rs", rs_h, rs),
    ]
    for i in range(4):
        at = pl.ds(4 * i, 4)
        parts.append(("basis%d" % i, basis_h.at[at], basis.at[at]))
    parts += [
        ("nt1", nt_h.at[0, 0, pl.ds(3, 5)], nt.at[pl.ds(3, 5)]),
        ("cond", cond_h, cond),
        ("nf", nf_h.at[0, 0], nf),
        ("linv", linv_h, linv),
        ("f0", f0_h.at[0, 0], f0),
    ]
    for i, (name, src, dst) in enumerate(parts):
        loads[name] = pltpu.make_async_copy(src, dst, lsem.at[i])
        loads[name].start()

    def send(src, dst, sends, recvs, who):
        copy = pltpu.make_async_remote_copy(
            src_ref=src, dst_ref=dst, send_sem=sends, recv_sem=recvs,
            device_id=who, device_id_type=MESH,
        )
        copy.start()
        return copy

    def send_group(src, buf, slot, peer):
        count = units()
        at, _ = offsets(count)
        for d in ORDER:
            n = count[d]
            send(
                src.at[pl.ds(0, n)], buf.at[pl.ds(at[d], n)], ssem.at[slot], rsem.at[slot], peer(d)
            )

    def send_all(src, buf, slot, peer):
        for d in ORDER:
            send(src, buf.at[d - 1], ssem.at[slot], rsem.at[slot], peer(d))

    def wait_bytes(buf, sem):
        pltpu.make_async_copy(buf, buf, sem).wait()

    def group_sums(src, buf):
        count = units()
        at, _ = offsets(count)
        out = []
        for unit in range(4):
            reach = [d for d in range(1, 16) if count[d] > unit]
            out.append(butterfly([src[unit]] + [buf[at[d] + unit] for d in reach]))
        return out

    def all_sums(src, buf, unit, size):
        terms = [src[unit]] + [buf[d, unit] for d in range(15)]
        return [butterfly(terms[i : i + size]) for i in range(0, 16, size)]

    def products(src, buf, unit, other, size):
        sums = all_sums(src, buf, unit, size)
        images = all_sums(src, buf, other, size)
        return sums[0], butterfly([s * m for s, m in zip(sums, images)])

    row = lax.broadcasted_iota(jnp.int32, (32, K), 0)
    lane = lax.broadcasted_iota(jnp.int32, (32, K), 1)

    def send_edges(t, rows_src, rows_buf, cols_src, cols_buf, first):
        first_row = jnp.concatenate([t[0:1], t[16:17]], axis=0)
        last_row = jnp.concatenate([t[15:16], t[31:32]], axis=0)
        rows_src[0] = jnp.where(even, last_row, first_row)
        rows_src[1] = jnp.where(even, first_row, last_row)
        lane8 = lane[0:8]
        last_col = pltpu.roll(t[0:8], 1, 1)
        first_col = t[0:8]
        for j in range(1, 4):
            part = t[8 * j : 8 * j + 8]
            last_col = jnp.where(lane8 == j, pltpu.roll(part, j + 1, 1), last_col)
            first_col = jnp.where(lane8 == j, pltpu.roll(part, j, 1), first_col)
        cols_src[0] = last_col
        cols_src[1] = first_col
        return [
            send(rows_src.at[0], rows_buf.at[0], hsem.at[first], hrsem.at[first], c_peer),
            send(rows_src.at[1], rows_buf.at[1], hsem.at[first + 1], hrsem.at[first + 1], (beyond, Z)),
            send(cols_src.at[0], cols_buf.at[0], hsem.at[first + 2], hrsem.at[first + 2], (X, z_up)),
            send(cols_src.at[1], cols_buf.at[1], hsem.at[first + 3], hrsem.at[first + 3], (X, z_down)),
        ]

    def beside(t, rows_buf, cols_buf, late=None):
        def spread(h):
            return jnp.concatenate(
                [jnp.broadcast_to(h[0:1], (16, K)), jnp.broadcast_to(h[1:2], (16, K))], axis=0
            )

        inside, outside = rows_buf[0], rows_buf[1]
        if late is not None:
            inside, outside = inside + late[0], outside + late[1]
        low = spread(jnp.where(X > 0, jnp.where(even, outside, inside), 0.0))
        high = spread(jnp.where(X < 31, jnp.where(even, inside, outside), 0.0))
        left, right = cols_buf[0], cols_buf[1]
        left = jnp.concatenate([left] + [pltpu.roll(left, K - j, 1) for j in range(1, 4)], axis=0)
        right = jnp.concatenate([pltpu.roll(right, K - 1 - j, 1) for j in range(4)], axis=0)
        if late is not None:
            left, right = left + late[2], right + late[3]
        left = jnp.where(Z > 0, left, 0.0)
        right = jnp.where(Z < 15, right, 0.0)
        return (
            jnp.where(row % 16 == 15, high, pltpu.roll(t, 31, 0)),
            jnp.where(row % 16 == 0, low, pltpu.roll(t, 1, 0)),
            jnp.where(lane == K - 1, right, pltpu.roll(t, K - 1, 1)),
            jnp.where(lane == 0, left, pltpu.roll(t, 1, 1)),
        )

    def flat_rows(ref):
        return jnp.concatenate([ref[:, x, :] for x in range(16)], axis=1)

    def coefficients(ref):
        return dot_w(flat_rows(ref), basis2[...])

    def leaf_apply(t):
        high, low = halves(shuffle(t))
        high, low = high.astype(F32), low.astype(F32)
        for i in range(16):
            j = 16 + i
            lhs = jnp.concatenate(
                [high[i : i + 1], high[j : j + 1], low[i : i + 1], low[j : j + 1]], axis=0
            )
            out = fold(jnp.dot(lhs.astype(BF16), linv2[i], preferred_element_type=F32))
            out = out[:, 0:K] + out[:, K:]
            tmp[pl.ds(i, 1)] = out[0:1]
            tmp[pl.ds(j, 1)] = out[1:2]
        return shuffle(tmp[...])

    def spread_out(y):
        lhs = both(y)
        w = fold(
            lax.dot_general(
                jnp.concatenate([lhs, lhs], axis=1), basis2[...],
                (((1,), (1,)), ((), ())), preferred_element_type=F32,
            )
        )
        for x in range(16):
            wt[:, x, :] = w[:, x * K : (x + 1) * K]
        return wt[...].reshape(32, K)

    def keep(ref, count, i, matrix):
        high, low = halves(matrix)
        ref[:, i * K : (i + 1) * K] = high
        ref[:, (count + i) * K : (count + i + 1) * K] = low

    def keep_down(h, matrix):
        high, low = halves(matrix)
        gs[h * K : (h + 1) * K, 0:K] = high
        gs[h * K : (h + 1) * K, K:] = low

    def put(ref, rows2, first=0):
        for i in range(rows2.shape[1] // K):
            ref[first + i] = rows2[:, i * K : (i + 1) * K]

    loads["e0"].wait()
    loads["nt0"].wait()
    p = e0[...]
    pf[0] = p
    keep(pa, 4, 3, p)
    for i in range(3):
        p = dot(p, nt[i])
        pf[i + 1] = p
        keep(pa, 4, 2 - i, p)
    loads["rs"].wait()
    for i in range(4):
        loads["basis%d" % i].wait()
        high, low = halves(basis[pl.ds(4 * i, 4)].reshape(4 * K, K))
        basis2[4 * K * i : 4 * K * (i + 1), 0:K] = high
        basis2[4 * K * i : 4 * K * (i + 1), K:] = low
    u0 = coefficients(rs)
    put(zs1, dot_w(u0, pa[...]))
    loads["nt1"].wait()
    r = nt[3]
    rf[0] = r
    keep(ra, 5, 4, r)
    for i in range(4):
        r = dot(r, nt[4 + i])
        rf[i + 1] = r
        keep(ra, 5, 3 - i, r)
    loads["nf"].wait()

    def image(h):
        return dot_t(dot_t(nf[h - 1], rf[h - 5]), pf[3])

    images = {h: image(h) for h in (6, 7, 8)}
    pl.semaphore_wait(barrier, len(others))
    send_group(zs1, zb1, 0, z_peer)

    images[9] = image(9)
    edge_rows = jnp.concatenate(
        [jnp.where(even, basis[15], basis[0]), jnp.where(even, basis[0], basis[15])], axis=0
    )
    edge_cols = jnp.concatenate([basis[:, K - 1, :], basis[:, 0, :]], axis=0)
    for h in range(6, 10):
        at = (h - 6) * K
        keep_down(h, images[h])
        of_rows = dot_t(images[h], edge_rows)
        hxs[0, at : at + K] = of_rows[:, 0:K]
        hxs[1, at : at + K] = of_rows[:, K:]
        of_cols = dot_t(edge_cols, images[h])
        hzs[0, :, at : at + K] = of_cols[0:16]
        hzs[1, :, at : at + K] = of_cols[16:]
    matrices = [
        send(hxs.at[0], hxb.at[0], msem.at[0], mrsem.at[0], c_peer),
        send(hxs.at[1], hxb.at[1], msem.at[1], mrsem.at[1], (beyond, Z)),
        send(hzs.at[0], hzb.at[0], msem.at[2], mrsem.at[2], (X, z_up)),
        send(hzs.at[1], hzb.at[1], msem.at[3], mrsem.at[3], (X, z_down)),
    ]
    loads["cond"].wait()
    k32 = tile_rows(cond[...])
    edges_k = send_edges(k32, krs, krb, kcs, kcb, 0)
    loads["linv"].wait()
    for i in range(16):
        high, low = halves(linv[i // 4, i % 4])
        linv2[i, :, 0:K] = high
        linv2[i, :, K:] = low
    b32 = rs[...].reshape(32, K)
    lb[...] = leaf_apply(b32)
    loads["f0"].wait()
    keep_down(0, f0[...])
    for h in range(1, 5):
        keep_down(h, dot_t(nf[h - 1], pf[h - 1]))
    keep_down(5, image(5))

    wait_bytes(zb1, rsem.at[0])
    u4, u3, u2, u1 = group_sums(zs1, zb1)
    put(cs1, dot_w(u4, ra[...]))
    core1 = send(cs1, cb1, ssem.at[1], rsem.at[1], c_peer)
    core1.wait_recv()
    u5 = cs1[4] + cb1[4]
    gs1[...] = cs1[pl.ds(0, 4)] + cb1[pl.ds(0, 4)]
    send_all(gs1, gb1, 2, g_peer)
    y = dot_w(jnp.concatenate([u0, u1, u2, u3, u4, u5], axis=1), gs[0 : 6 * K])
    z = lb[...] + spread_out(y)
    edges_z = send_edges(z, hrs, hrb, hcs, hcb, 4)
    for h in range(1, 4):
        keep(pb, 4, 3 - h, dot(pf[h - 1], nf[h - 1]))
    keep(pb, 4, 3, f0[...])
    for h in range(5, 10):
        keep(rb, 6, 9 - h, dot(rf[h - 5], nf[h - 1]))
    keep(rb, 6, 5, nf[3])
    for e in edges_k:
        e.wait_recv()
    weights = [0.5 * (k32 + other) for other in beside(k32, krb, kcb)]
    for m in matrices:
        m.wait_recv()
    for side in range(2):
        high, low = halves(hxb[side])
        hx2[side, :, 0:K] = high
        hx2[side, :, K:] = low
        high, low = halves(hzb[side])
        hz2[16 * side : 16 * side + 16] = high
        hz2[32 + 16 * side : 48 + 16 * side] = low
    for e in edges_z:
        e.wait_recv()
    wait_bytes(gb1, rsem.at[2])
    u9 = all_sums(gs1, gb1, 0, 16)[0]
    all8, all7, all6 = [all_sums(gs1, gb1, 4 - n, 2**n) for n in (3, 2, 1)]
    mine = jnp.concatenate([all6[0], all7[0], all8[0], u9], axis=1)
    apart = (X // 2) ^ (beyond // 2)
    theirs6 = jnp.where(
        apart == 15, all6[7], jnp.where(apart == 7, all6[3], jnp.where(apart == 3, all6[1], all6[0]))
    )
    theirs7 = jnp.where(apart == 15, all7[3], jnp.where(apart == 7, all7[1], all7[0]))
    theirs8 = jnp.where(apart == 15, all8[1], all8[0])
    theirs = jnp.concatenate([theirs6, theirs7, theirs8, u9], axis=1)
    z = z + spread_out(dot_w(mine, gs[6 * K : 10 * K]))
    cols = fold(
        lax.dot_general(
            hz2[...], both(mine), (((1,), (1,)), ((), ())), preferred_element_type=F32
        )
    )
    cols = cols[:, 0:2] + cols[:, 2:4]

    def column(side):
        part = cols[16 * side : 16 * side + 16]
        return jnp.concatenate(
            [jnp.broadcast_to(part[:, i : i + 1], (16, K)) for i in range(2)], axis=0
        )

    late = (dot_w(mine, hx2[0]), dot_w(theirs, hx2[1]), column(0), column(1))
    applied = jnp.zeros_like(z)
    for weight, other in zip(weights, beside(z, hrb, hcb, late)):
        applied = applied + weight * (z - other)
    wt[...] = applied.reshape(2, 16, K)

    lane2 = lane[0:2]

    def columns(t):
        return jnp.sum(t.reshape(2, 16, K), axis=1)

    def quadratic(t):
        return jnp.where(lane2 >= 64, t + pltpu.roll(t, 64, 1), 0.0)

    u0 = coefficients(wt)
    put(zs2, dot_w(u0, pa[...]), 1)
    low = dot_w(u0, pb[...])
    put(zs2, low[:, 0 : 3 * K], 5)
    near = leaf_apply(applied)
    inner = jnp.concatenate([columns(b32 * z), columns(z * applied)], axis=0)
    inner = inner + pltpu.roll(inner, 64, 1)
    inner = inner + pltpu.roll(inner, 32, 1)
    zs2[0] = jnp.where(lane2 < 32, inner[0:2], jnp.where(lane2 < 64, inner[2:4], 0.0)) + quadratic(
        columns(applied * near) + u0 * low[:, 3 * K :]
    )
    send_all(zs2, zb2, 3, z_peer)
    wait_bytes(zb2, rsem.at[3])
    u4 = all_sums(zs2, zb2, 1, 16)[0]
    up = dot_w(u4, ra[...])
    mapped_up = dot_w(u4, rb[...])
    u3, q3 = products(zs2, zb2, 2, 5, 8)
    u2, q2 = products(zs2, zb2, 3, 6, 4)
    u1, q1 = products(zs2, zb2, 4, 7, 2)
    cs2[0] = all_sums(zs2, zb2, 0, 16)[0] + quadratic(q1 + q2 + q3 + u4 * mapped_up[:, 5 * K :])
    put(cs2, up[:, 0 : 4 * K], 1)
    put(cs2, mapped_up[:, 0 : 4 * K], 5)
    cs2[9] = up[:, 4 * K :]
    cs2[10] = mapped_up[:, 4 * K : 5 * K]
    core2 = send(cs2, cb2, ssem.at[4], rsem.at[4], c_peer)
    core2.wait_recv()
    u5 = cs2[9] + cb2[9]
    gs2[...] = cs2[pl.ds(0, 9)] + cb2[pl.ds(0, 9)]
    gs2[0] = gs2[0] + quadratic(u5 * (cs2[10] + cb2[10]))
    send_all(gs2, gb2, 5, g_peer)
    y = dot_w(jnp.concatenate([u0, u1, u2, u3, u4, u5], axis=1), gs[0 : 6 * K])
    for e in edges_k + edges_z + matrices + [core1, core2]:
        e.wait_send()
    for buf, slot in ((zb1, 0), (gb1, 2), (zb2, 3)):
        wait_bytes(buf, ssem.at[slot])
    wait_bytes(gb2, rsem.at[5])
    u9, q9 = products(gs2, gb2, 1, 5, 16)
    u8, q8 = products(gs2, gb2, 2, 6, 8)
    u7, q7 = products(gs2, gb2, 3, 7, 4)
    u6, q6 = products(gs2, gb2, 4, 8, 2)
    inner = all_sums(gs2, gb2, 0, 16)[0] + quadratic(q6 + q7 + q8 + q9)

    def over_lanes(t):
        return jnp.sum(t, axis=1, keepdims=True)

    rz_old = over_lanes(jnp.where(lane2 < 32, inner, 0.0))
    curvature = over_lanes(jnp.where((lane2 >= 32) & (lane2 < 64), inner, 0.0))
    squared = over_lanes(jnp.where(lane2 >= 64, inner, 0.0))
    step = rz_old / curvature
    rz_new = rz_old - 2.0 * step * curvature + step * step * squared

    def over_tile(t):
        return jnp.concatenate(
            [jnp.broadcast_to(t[0:1], (16, K)), jnp.broadcast_to(t[1:2], (16, K))], axis=0
        )

    step32 = over_tile(step)
    out[0:2] = (step32 * z).reshape(2, 16, K)
    out[2:4] = (b32 - step32 * applied).reshape(2, 16, K)
    results = [pltpu.make_async_copy(out.at[pl.ds(0, 4)], out_o.at[pl.ds(0, 4)], lsem.at[0])]
    results[0].start()
    y = y + dot_w(jnp.concatenate([u6, u7, u8, u9], axis=1), gs[6 * K : 10 * K])
    mapped = near + spread_out(y)
    second = z - step32 * mapped
    out[4:6] = (second + over_tile(rz_new / rz_old) * z).reshape(2, 16, K)
    results.append(pltpu.make_async_copy(out.at[pl.ds(4, 2)], out_o.at[pl.ds(4, 2)], lsem.at[1]))
    results[1].start()

    wait_bytes(gb2, ssem.at[5])
    for part in results:
        part.wait()


def on_device(*args):
    unit = lambda *n: pltpu.VMEM(n + (2, K), F32)
    square = lambda *n: pltpu.VMEM(n + (K, K), F32)
    out = pl.pallas_call(
        kernel,
        name="pcg_step",
        out_shape=jax.ShapeDtypeStruct((6, 16, K), F32),
        in_specs=[pl.BlockSpec(memory_space=pl.ANY)] * 8,
        out_specs=pl.BlockSpec(memory_space=pl.ANY),
        scratch_shapes=[
            pltpu.VMEM((2, 16, K), F32), pltpu.VMEM((16, K), F32), square(4, 4), square(16),
            square(), square(8), square(), square(9),
            square(4), square(5), pltpu.VMEM((16 * K, 2 * K), BF16), pltpu.VMEM((16, K, 2 * K), BF16),
            pltpu.VMEM((K, 8 * K), BF16), pltpu.VMEM((K, 8 * K), BF16),
            pltpu.VMEM((K, 10 * K), BF16), pltpu.VMEM((K, 12 * K), BF16),
            pltpu.VMEM((10 * K, 2 * K), BF16),
            pltpu.VMEM((32, K), F32), pltpu.VMEM((2, 16, K), F32), pltpu.VMEM((32, K), F32),
            unit(4), unit(26), unit(8), unit(15, 8), unit(5), unit(5), unit(11), unit(11),
            unit(4), unit(15, 4), unit(9), unit(15, 9),
            unit(2), unit(2), pltpu.VMEM((2, 8, K), F32), pltpu.VMEM((2, 8, K), F32),
            unit(2), unit(2), pltpu.VMEM((2, 8, K), F32), pltpu.VMEM((2, 8, K), F32),
            pltpu.VMEM((2, 4 * K, K), F32), pltpu.VMEM((2, 4 * K, K), F32),
            pltpu.VMEM((2, 4 * K, 2 * K), BF16),
            pltpu.VMEM((2, 16, 4 * K), F32), pltpu.VMEM((2, 16, 4 * K), F32),
            pltpu.VMEM((64, 4 * K), BF16), pltpu.VMEM((6, 16, K), F32),
            pltpu.SemaphoreType.DMA((12,)), pltpu.SemaphoreType.DMA((6,)),
            pltpu.SemaphoreType.DMA((6,)), pltpu.SemaphoreType.DMA((8,)),
            pltpu.SemaphoreType.DMA((8,)), pltpu.SemaphoreType.DMA((4,)),
            pltpu.SemaphoreType.DMA((4,)),
        ],
        compiler_params=pltpu.CompilerParams(
            collective_id=0, has_side_effects=True, vmem_limit_bytes=60 * 1024 * 1024
        ),
    )(*args)
    return out[0:2], out[2:4], out[4:6]


def solution(mesh):
    return jax.shard_map(
        on_device,
        mesh=mesh,
        in_specs=(
            P(None, "gx", "gy"),
            P("gx", "gy"),
            P("gx", "gy", None, None),
            P("gx", "gy", None),
            P("gx", "gy", None, None),
            P("gx", "gy", None, None, None),
            P("gx", "gy", None, None),
            P("gx", "gy", None, None, None),
        ),
        out_specs=(P(None, "gx", "gy"), P(None, "gx", "gy"), P(None, "gx", "gy")),
        check_vma=False,
    )
```

```python
import jax
import jax.numpy as jnp
from jax import lax
from jax.experimental import pallas as pl
from jax.experimental.pallas import tpu as pltpu
from jax.sharding import PartitionSpec as P

HIGHEST = lax.Precision.HIGHEST
MESH = pl.DeviceIdType.MESH
F32 = jnp.float32
BF16 = jnp.bfloat16
K = 128


def dot(a, b):
    return lax.dot_general(
        a, b, (((1,), (0,)), ((), ())), precision=HIGHEST, preferred_element_type=F32
    )


def dot_t(a, b):
    return lax.dot_general(
        a, b, (((1,), (1,)), ((), ())), precision=HIGHEST, preferred_element_type=F32
    )


def halves(a):
    high = a.astype(BF16)
    return high, (a - high.astype(F32)).astype(BF16)


def both(a):
    return jnp.concatenate(halves(a), axis=0)


def fold(out):
    n = out.shape[0] // 2
    return out[0:n] + out[n:]


def dot_w(a, w):
    n = w.shape[1] // 2
    out = fold(jnp.dot(both(a), w, preferred_element_type=F32))
    return out[:, 0:n] + out[:, n:]


def units():
    return {d: 5 - d.bit_length() for d in range(1, 16)}


def offsets(count):
    at, out = 0, {}
    for d in sorted(count):
        out[d] = at
        at += count[d]
    return out, at


def butterfly(values):
    while len(values) > 1:
        values = [values[i] + values[i + 1] for i in range(0, len(values), 2)]
    return values[0]


ORDER = (8, 15, 14, 13, 12, 11, 10, 9, 7, 6, 5, 4, 3, 2, 1)


def tile_rows(x):
    return jnp.concatenate([x, x], axis=0)


def shuffle(t):
    row = lax.broadcasted_iota(jnp.int32, t.shape, 0) % 4
    chunk = lax.broadcasted_iota(jnp.int32, t.shape, 1) // 32
    rows, lanes = t.shape
    out = t
    for delta in (-3, -2, -1, 1, 2, 3):
        moved = pltpu.roll(t, delta % rows, 0)
        moved = pltpu.roll(moved, (-32 * delta) % lanes, 1)
        out = jnp.where(row - chunk == delta, moved, out)
    return out


def kernel(
    rs_h, cond_h, linv_h, basis_h, e0_h, nt_h, f0_h, nf_h,
    out_o,
    rs, cond, linv, basis, e0, nt, f0, nf,
    pf, rf, basis2, linv2, pa, pb, ra, rb, gs, lb, wt, tmp,
    zs1, zb1, zs2, zb2, zx2, cs1, cb1, cs2, cb2, gs1, gb1, gs2, gb2,
    hrs, hrb, hcs, hcb, krs, krb, kcs, kcb,
    hxs, hxb, hx2, hzs, hzb, hz2,
    lsem, ssem, rsem, hsem, hrsem, msem, mrsem,
):
    X = lax.axis_index("gx")
    Z = lax.axis_index("gy")
    z_peer = lambda d: (X, Z ^ d)
    c_peer = (X ^ 1, Z)
    g_peer = lambda d: (X ^ (2 * d), Z)
    even = X % 2 == 0
    beyond = (X + 31 + 2 * (X % 2)) % 32
    z_up, z_down = (Z + 1) % 16, (Z + 15) % 16

    barrier = pltpu.get_barrier_semaphore()
    others = [z_peer(d) for d in ORDER] + [g_peer(d) for d in ORDER] + [c_peer]
    others.append((beyond, Z))
    for who in others:
        pl.semaphore_signal(barrier, inc=1, device_id=who, device_id_type=MESH)

    loads = {}
    parts = [
        ("e0", e0_h.at[0, 0], e0),
        ("nt0", nt_h.at[0, 0, pl.ds(0, 3)], nt.at[pl.ds(0, 3)]),
        ("rs", rs_h, rs),
    ]
    for i in range(4):
        at = pl.ds(4 * i, 4)
        parts.append(("basis%d" % i, basis_h.at[at], basis.at[at]))
    parts += [
        ("nt1", nt_h.at[0, 0, pl.ds(3, 5)], nt.at[pl.ds(3, 5)]),
        ("cond", cond_h, cond),
        ("nf", nf_h.at[0, 0], nf),
        ("linv", linv_h, linv),
        ("f0", f0_h.at[0, 0], f0),
    ]
    for i, (name, src, dst) in enumerate(parts):
        loads[name] = pltpu.make_async_copy(src, dst, lsem.at[i])
        loads[name].start()

    def send(src, dst, sends, recvs, who):
        copy = pltpu.make_async_remote_copy(
            src_ref=src, dst_ref=dst, send_sem=sends, recv_sem=recvs,
            device_id=who, device_id_type=MESH,
        )
        copy.start()
        return copy

    def send_group(src, buf, slot, peer):
        count = units()
        at, _ = offsets(count)
        for d in ORDER:
            n = count[d]
            send(
                src.at[pl.ds(0, n)], buf.at[pl.ds(at[d], n)], ssem.at[slot], rsem.at[slot], peer(d)
            )

    def send_all(src, buf, slot, peer):
        for d in ORDER:
            send(src, buf.at[d - 1], ssem.at[slot], rsem.at[slot], peer(d))

    def wait_bytes(buf, sem):
        pltpu.make_async_copy(buf, buf, sem).wait()

    def group_sums(src, buf):
        count = units()
        at, _ = offsets(count)
        out = []
        for unit in range(4):
            reach = [d for d in range(1, 16) if count[d] > unit]
            out.append(butterfly([src[unit]] + [buf[at[d] + unit] for d in reach]))
        return out

    def all_sums(src, buf, unit, size):
        terms = [src[unit]] + [buf[d, unit] for d in range(15)]
        return [butterfly(terms[i : i + size]) for i in range(0, 16, size)]

    def products(src, buf, unit, other, size):
        sums = all_sums(src, buf, unit, size)
        images = all_sums(src, buf, other, size)
        return sums[0], butterfly([s * m for s, m in zip(sums, images)])

    row = lax.broadcasted_iota(jnp.int32, (32, K), 0)
    lane = lax.broadcasted_iota(jnp.int32, (32, K), 1)

    def send_edges(t, rows_src, rows_buf, cols_src, cols_buf, first):
        first_row = jnp.concatenate([t[0:1], t[16:17]], axis=0)
        last_row = jnp.concatenate([t[15:16], t[31:32]], axis=0)
        rows_src[0] = jnp.where(even, last_row, first_row)
        rows_src[1] = jnp.where(even, first_row, last_row)
        lane8 = lane[0:8]
        last_col = pltpu.roll(t[0:8], 1, 1)
        first_col = t[0:8]
        for j in range(1, 4):
            part = t[8 * j : 8 * j + 8]
            last_col = jnp.where(lane8 == j, pltpu.roll(part, j + 1, 1), last_col)
            first_col = jnp.where(lane8 == j, pltpu.roll(part, j, 1), first_col)
        cols_src[0] = last_col
        cols_src[1] = first_col
        return [
            send(rows_src.at[0], rows_buf.at[0], hsem.at[first], hrsem.at[first], c_peer),
            send(rows_src.at[1], rows_buf.at[1], hsem.at[first + 1], hrsem.at[first + 1], (beyond, Z)),
            send(cols_src.at[0], cols_buf.at[0], hsem.at[first + 2], hrsem.at[first + 2], (X, z_up)),
            send(cols_src.at[1], cols_buf.at[1], hsem.at[first + 3], hrsem.at[first + 3], (X, z_down)),
        ]

    def beside(t, rows_buf, cols_buf, late=None):
        def spread(h):
            return jnp.concatenate(
                [jnp.broadcast_to(h[0:1], (16, K)), jnp.broadcast_to(h[1:2], (16, K))], axis=0
            )

        inside, outside = rows_buf[0], rows_buf[1]
        if late is not None:
            inside, outside = inside + late[0], outside + late[1]
        low = spread(jnp.where(X > 0, jnp.where(even, outside, inside), 0.0))
        high = spread(jnp.where(X < 31, jnp.where(even, inside, outside), 0.0))
        left, right = cols_buf[0], cols_buf[1]
        left = jnp.concatenate([left] + [pltpu.roll(left, K - j, 1) for j in range(1, 4)], axis=0)
        right = jnp.concatenate([pltpu.roll(right, K - 1 - j, 1) for j in range(4)], axis=0)
        if late is not None:
            left, right = left + late[2], right + late[3]
        left = jnp.where(Z > 0, left, 0.0)
        right = jnp.where(Z < 15, right, 0.0)
        return (
            jnp.where(row % 16 == 15, high, pltpu.roll(t, 31, 0)),
            jnp.where(row % 16 == 0, low, pltpu.roll(t, 1, 0)),
            jnp.where(lane == K - 1, right, pltpu.roll(t, K - 1, 1)),
            jnp.where(lane == 0, left, pltpu.roll(t, 1, 1)),
        )

    def flat_rows(ref):
        return jnp.concatenate([ref[:, x, :] for x in range(16)], axis=1)

    def coefficients(ref):
        return dot_w(flat_rows(ref), basis2[...])

    def leaf_apply(t):
        high, low = halves(shuffle(t))
        high, low = high.astype(F32), low.astype(F32)
        for i in range(16):
            j = 16 + i
            lhs = jnp.concatenate(
                [high[i : i + 1], high[j : j + 1], low[i : i + 1], low[j : j + 1]], axis=0
            )
            out = fold(jnp.dot(lhs.astype(BF16), linv2[i], preferred_element_type=F32))
            out = out[:, 0:K] + out[:, K:]
            tmp[pl.ds(i, 1)] = out[0:1]
            tmp[pl.ds(j, 1)] = out[1:2]
        return shuffle(tmp[...])

    def spread_out(y):
        lhs = both(y)
        w = fold(
            lax.dot_general(
                jnp.concatenate([lhs, lhs], axis=1), basis2[...],
                (((1,), (1,)), ((), ())), preferred_element_type=F32,
            )
        )
        for x in range(16):
            wt[:, x, :] = w[:, x * K : (x + 1) * K]
        return wt[...].reshape(32, K)

    def keep(ref, count, i, matrix):
        high, low = halves(matrix)
        ref[:, i * K : (i + 1) * K] = high
        ref[:, (count + i) * K : (count + i + 1) * K] = low

    def keep_down(h, matrix):
        high, low = halves(matrix)
        gs[h * K : (h + 1) * K, 0:K] = high
        gs[h * K : (h + 1) * K, K:] = low

    def put(ref, rows2, first=0):
        for i in range(rows2.shape[1] // K):
            ref[first + i] = rows2[:, i * K : (i + 1) * K]

    loads["e0"].wait()
    loads["nt0"].wait()
    p = e0[...]
    pf[0] = p
    keep(pa, 4, 3, p)
    for i in range(3):
        p = dot(p, nt[i])
        pf[i + 1] = p
        keep(pa, 4, 2 - i, p)
    loads["rs"].wait()
    for i in range(4):
        loads["basis%d" % i].wait()
        high, low = halves(basis[pl.ds(4 * i, 4)].reshape(4 * K, K))
        basis2[4 * K * i : 4 * K * (i + 1), 0:K] = high
        basis2[4 * K * i : 4 * K * (i + 1), K:] = low
    u0 = coefficients(rs)
    put(zs1, dot_w(u0, pa[...]))
    loads["nt1"].wait()
    r = nt[3]
    rf[0] = r
    keep(ra, 5, 4, r)
    for i in range(4):
        r = dot(r, nt[4 + i])
        rf[i + 1] = r
        keep(ra, 5, 3 - i, r)
    loads["nf"].wait()

    def image(h):
        return dot_t(dot_t(nf[h - 1], rf[h - 5]), pf[3])

    images = {h: image(h) for h in (6, 7, 8)}
    pl.semaphore_wait(barrier, len(others))
    send_group(zs1, zb1, 0, z_peer)

    images[9] = image(9)
    edge_rows = jnp.concatenate(
        [jnp.where(even, basis[15], basis[0]), jnp.where(even, basis[0], basis[15])], axis=0
    )
    edge_cols = jnp.concatenate([basis[:, K - 1, :], basis[:, 0, :]], axis=0)
    for h in range(6, 10):
        at = (h - 6) * K
        keep_down(h, images[h])
        of_rows = dot_t(images[h], edge_rows)
        hxs[0, at : at + K] = of_rows[:, 0:K]
        hxs[1, at : at + K] = of_rows[:, K:]
        of_cols = dot_t(edge_cols, images[h])
        hzs[0, :, at : at + K] = of_cols[0:16]
        hzs[1, :, at : at + K] = of_cols[16:]
    matrices = [
        send(hxs.at[0], hxb.at[0], msem.at[0], mrsem.at[0], c_peer),
        send(hxs.at[1], hxb.at[1], msem.at[1], mrsem.at[1], (beyond, Z)),
        send(hzs.at[0], hzb.at[0], msem.at[2], mrsem.at[2], (X, z_up)),
        send(hzs.at[1], hzb.at[1], msem.at[3], mrsem.at[3], (X, z_down)),
    ]
    loads["cond"].wait()
    k32 = tile_rows(cond[...])
    edges_k = send_edges(k32, krs, krb, kcs, kcb, 0)
    loads["linv"].wait()
    for i in range(16):
        high, low = halves(linv[i // 4, i % 4])
        linv2[i, :, 0:K] = high
        linv2[i, :, K:] = low
    b32 = rs[...].reshape(32, K)
    lb[...] = leaf_apply(b32)
    loads["f0"].wait()
    keep_down(0, f0[...])
    for h in range(1, 5):
        keep_down(h, dot_t(nf[h - 1], pf[h - 1]))
    keep_down(5, image(5))

    wait_bytes(zb1, rsem.at[0])
    u4, u3, u2, u1 = group_sums(zs1, zb1)
    put(cs1, dot_w(u4, ra[...]))
    core1 = send(cs1, cb1, ssem.at[1], rsem.at[1], c_peer)
    core1.wait_recv()
    u5 = cs1[4] + cb1[4]
    gs1[...] = cs1[pl.ds(0, 4)] + cb1[pl.ds(0, 4)]
    send_all(gs1, gb1, 2, g_peer)
    y = dot_w(jnp.concatenate([u0, u1, u2, u3, u4, u5], axis=1), gs[0 : 6 * K])
    z = lb[...] + spread_out(y)
    edges_z = send_edges(z, hrs, hrb, hcs, hcb, 4)
    for h in range(1, 4):
        keep(pb, 4, 3 - h, dot(pf[h - 1], nf[h - 1]))
    keep(pb, 4, 3, f0[...])
    for h in range(5, 10):
        keep(rb, 6, 9 - h, dot(rf[h - 5], nf[h - 1]))
    keep(rb, 6, 5, nf[3])
    for e in edges_k:
        e.wait_recv()
    weights = [0.5 * (k32 + other) for other in beside(k32, krb, kcb)]
    for m in matrices:
        m.wait_recv()
    for side in range(2):
        high, low = halves(hxb[side])
        hx2[side, :, 0:K] = high
        hx2[side, :, K:] = low
        high, low = halves(hzb[side])
        hz2[16 * side : 16 * side + 16] = high
        hz2[32 + 16 * side : 48 + 16 * side] = low
    for e in edges_z:
        e.wait_recv()
    wait_bytes(gb1, rsem.at[2])
    u9 = all_sums(gs1, gb1, 0, 16)[0]
    all8, all7, all6 = [all_sums(gs1, gb1, 4 - n, 2**n) for n in (3, 2, 1)]
    mine = jnp.concatenate([all6[0], all7[0], all8[0], u9], axis=1)
    apart = (X // 2) ^ (beyond // 2)
    theirs6 = jnp.where(
        apart == 15, all6[7], jnp.where(apart == 7, all6[3], jnp.where(apart == 3, all6[1], all6[0]))
    )
    theirs7 = jnp.where(apart == 15, all7[3], jnp.where(apart == 7, all7[1], all7[0]))
    theirs8 = jnp.where(apart == 15, all8[1], all8[0])
    theirs = jnp.concatenate([theirs6, theirs7, theirs8, u9], axis=1)
    z = z + spread_out(dot_w(mine, gs[6 * K : 10 * K]))
    cols = fold(
        lax.dot_general(
            hz2[...], both(mine), (((1,), (1,)), ((), ())), preferred_element_type=F32
        )
    )
    cols = cols[:, 0:2] + cols[:, 2:4]

    def column(side):
        part = cols[16 * side : 16 * side + 16]
        return jnp.concatenate(
            [jnp.broadcast_to(part[:, i : i + 1], (16, K)) for i in range(2)], axis=0
        )

    late = (dot_w(mine, hx2[0]), dot_w(theirs, hx2[1]), column(0), column(1))
    applied = jnp.zeros_like(z)
    for weight, other in zip(weights, beside(z, hrb, hcb, late)):
        applied = applied + weight * (z - other)
    wt[...] = applied.reshape(2, 16, K)

    lane2 = lane[0:2]

    def columns(t):
        return jnp.sum(t.reshape(2, 16, K), axis=1)

    def quadratic(t):
        return jnp.where(lane2 >= 64, t + pltpu.roll(t, 64, 1), 0.0)

    u0 = coefficients(wt)
    put(zs2, dot_w(u0, pa[...]), 1)
    low = dot_w(u0, pb[...])
    put(zs2, low[:, 0 : 2 * K], 5)
    m1, image1 = zs2[4], low[:, 2 * K : 3 * K]
    zs2[4] = jnp.where(Z % 2 == 0, m1, image1)
    zs2[7] = m1
    near = leaf_apply(applied)
    inner = jnp.concatenate([columns(b32 * z), columns(z * applied)], axis=0)
    inner = inner + pltpu.roll(inner, 64, 1)
    inner = inner + pltpu.roll(inner, 32, 1)
    zs2[0] = jnp.where(lane2 < 32, inner[0:2], jnp.where(lane2 < 64, inner[2:4], 0.0)) + quadratic(
        columns(applied * near) + u0 * low[:, 3 * K :] + m1 * image1
    )
    for d in ORDER:
        send(zs2.at[pl.ds(0, 7)], zb2.at[d - 1], ssem.at[3], rsem.at[3], z_peer(d))
    pair = send(zs2.at[pl.ds(7, 1)], zx2, ssem.at[6], rsem.at[6], z_peer(1))
    wait_bytes(zb2, rsem.at[3])
    u4 = all_sums(zs2, zb2, 1, 16)[0]
    up = dot_w(u4, ra[...])
    mapped_up = dot_w(u4, rb[...])
    u3, q3 = products(zs2, zb2, 2, 5, 8)
    u2, q2 = products(zs2, zb2, 3, 6, 4)
    pair.wait_recv()
    u1 = zs2[7] + zx2[0]
    terms = [zs2[4]] + [zb2[d, 4] for d in range(15)]
    q1 = 2.0 * butterfly([terms[i] * terms[i + 1] for i in range(0, 16, 2)])
    cs2[0] = all_sums(zs2, zb2, 0, 16)[0] + quadratic(q1 + q2 + q3 + u4 * mapped_up[:, 5 * K :])
    put(cs2, up[:, 0 : 4 * K], 1)
    put(cs2, mapped_up[:, 0 : 4 * K], 5)
    cs2[9] = up[:, 4 * K :]
    cs2[10] = mapped_up[:, 4 * K : 5 * K]
    core2 = send(cs2, cb2, ssem.at[4], rsem.at[4], c_peer)
    core2.wait_recv()
    u5 = cs2[9] + cb2[9]
    gs2[...] = cs2[pl.ds(0, 9)] + cb2[pl.ds(0, 9)]
    gs2[0] = gs2[0] + quadratic(u5 * (cs2[10] + cb2[10]))
    send_all(gs2, gb2, 5, g_peer)
    y = dot_w(jnp.concatenate([u0, u1, u2, u3, u4, u5], axis=1), gs[0 : 6 * K])
    wait_bytes(gb2, rsem.at[5])
    u9, q9 = products(gs2, gb2, 1, 5, 16)
    u8, q8 = products(gs2, gb2, 2, 6, 8)
    u7, q7 = products(gs2, gb2, 3, 7, 4)
    u6, q6 = products(gs2, gb2, 4, 8, 2)
    y = y + dot_w(jnp.concatenate([u6, u7, u8, u9], axis=1), gs[6 * K : 10 * K])
    mapped = near + spread_out(y)
    inner = all_sums(gs2, gb2, 0, 16)[0] + quadratic(q6 + q7 + q8 + q9)

    def over_lanes(t):
        return jnp.sum(t, axis=1, keepdims=True)

    rz_old = over_lanes(jnp.where(lane2 < 32, inner, 0.0))
    curvature = over_lanes(jnp.where((lane2 >= 32) & (lane2 < 64), inner, 0.0))
    squared = over_lanes(jnp.where(lane2 >= 64, inner, 0.0))
    step = rz_old / curvature
    rz_new = rz_old - 2.0 * step * curvature + step * step * squared

    def over_tile(t):
        return jnp.concatenate(
            [jnp.broadcast_to(t[0:1], (16, K)), jnp.broadcast_to(t[1:2], (16, K))], axis=0
        )

    step32 = over_tile(step)
    out_o[0:2] = (step32 * z).reshape(2, 16, K)
    out_o[2:4] = (b32 - step32 * applied).reshape(2, 16, K)
    second = z - step32 * mapped
    out_o[4:6] = (second + over_tile(rz_new / rz_old) * z).reshape(2, 16, K)

    for e in edges_k + edges_z + matrices + [core1, core2, pair]:
        e.wait_send()
    for buf, slot in ((zb1, 0), (gb1, 2), (zb2, 3), (gb2, 5)):
        wait_bytes(buf, ssem.at[slot])


def on_device(*args):
    unit = lambda *n: pltpu.VMEM(n + (2, K), F32)
    square = lambda *n: pltpu.VMEM(n + (K, K), F32)
    out = pl.pallas_call(
        kernel,
        name="pcg_step",
        out_shape=jax.ShapeDtypeStruct((6, 16, K), F32),
        in_specs=[pl.BlockSpec(memory_space=pl.ANY)] * 8,
        out_specs=pl.BlockSpec(memory_space=pltpu.VMEM),
        scratch_shapes=[
            pltpu.VMEM((2, 16, K), F32), pltpu.VMEM((16, K), F32), square(4, 4), square(16),
            square(), square(8), square(), square(9),
            square(4), square(5), pltpu.VMEM((16 * K, 2 * K), BF16), pltpu.VMEM((16, K, 2 * K), BF16),
            pltpu.VMEM((K, 8 * K), BF16), pltpu.VMEM((K, 8 * K), BF16),
            pltpu.VMEM((K, 10 * K), BF16), pltpu.VMEM((K, 12 * K), BF16),
            pltpu.VMEM((10 * K, 2 * K), BF16),
            pltpu.VMEM((32, K), F32), pltpu.VMEM((2, 16, K), F32), pltpu.VMEM((32, K), F32),
            unit(4), unit(26), unit(8), unit(15, 7), unit(1), unit(5), unit(5), unit(11), unit(11),
            unit(4), unit(15, 4), unit(9), unit(15, 9),
            unit(2), unit(2), pltpu.VMEM((2, 8, K), F32), pltpu.VMEM((2, 8, K), F32),
            unit(2), unit(2), pltpu.VMEM((2, 8, K), F32), pltpu.VMEM((2, 8, K), F32),
            pltpu.VMEM((2, 4 * K, K), F32), pltpu.VMEM((2, 4 * K, K), F32),
            pltpu.VMEM((2, 4 * K, 2 * K), BF16),
            pltpu.VMEM((2, 16, 4 * K), F32), pltpu.VMEM((2, 16, 4 * K), F32),
            pltpu.VMEM((64, 4 * K), BF16),
            pltpu.SemaphoreType.DMA((12,)), pltpu.SemaphoreType.DMA((7,)),
            pltpu.SemaphoreType.DMA((7,)), pltpu.SemaphoreType.DMA((8,)),
            pltpu.SemaphoreType.DMA((8,)), pltpu.SemaphoreType.DMA((4,)),
            pltpu.SemaphoreType.DMA((4,)),
        ],
        compiler_params=pltpu.CompilerParams(
            collective_id=0, has_side_effects=True, vmem_limit_bytes=60 * 1024 * 1024
        ),
    )(*args)
    return out[0:2], out[2:4], out[4:6]


def solution(mesh):
    return jax.shard_map(
        on_device,
        mesh=mesh,
        in_specs=(
            P(None, "gx", "gy"),
            P("gx", "gy"),
            P("gx", "gy", None, None),
            P("gx", "gy", None),
            P("gx", "gy", None, None),
            P("gx", "gy", None, None, None),
            P("gx", "gy", None, None),
            P("gx", "gy", None, None, None),
        ),
        out_specs=(P(None, "gx", "gy"), P(None, "gx", "gy"), P(None, "gx", "gy")),
        check_vma=False,
    )
```
